128 devices in a mesh: dp: 8 (over y, core), tensor: 16 (over z, x).
Axes of the slice: x: 4, y: 4, z: 4, core: 2. Of those that a mesh axis runs over, the one named last changes fastest.
Arguments:
- hidden: bfloat16 [4096, 1536], P(('dp', 'tensor')), may hold values from -6 to 6
- norm_gain: float32 [1536], replicated, may hold values from 0.25 to 1.75
- unembed: bfloat16 [1536, 77824], P(None, 'tensor'), may hold values from -0.15625 to 0.15625
- verifier_logits: bfloat16 [4096, 77824], P('dp', 'tensor'), may hold values from -4 to 340
- served_ids: int32 [4096], P('dp'), may hold values from 0 to 77823
- accepted: int32 [512], P('dp'), may hold values from 0 to 8
Outputs:
- grad_unembed: bfloat16 [1536, 77824], P('dp', 'tensor')
- grad_hidden: bfloat16 [4096, 1536], P(('dp', 'tensor'))
The draws below stay inside these ranges and needn't reach their ends.
All inputs are finite; a program needn't handle non-finite values.
Results may differ from the reference program's by a relative error of at most 0.02.
Values may be sent and summed in bfloat16 or wider, within the bound.
A program may use at most 128 MiB of HBM per device.

```python
import math
import jax
import jax.numpy as jnp
import numpy as np
from jax import lax

D = 1536
V = 77824
DRAFT = 8
ROWS = 4096
BLOCKS = 512
N_DP = 8


def draw_verifier_logits(key, part):
    key = jax.random.fold_in(key, 11)
    key_base = jax.random.fold_in(key, 0)
    base = jnp.clip(0.8 * jax.random.normal(key_base, (ROWS, V), jnp.float32), -3.5, 3.5)
    return base.astype(jnp.bfloat16)


def set_ends(array, own_key, smallest, largest):
    longest = array.shape.index(max(array.shape))
    spots = []
    for shift in (0, 1):
        where = [jax.random.randint(jax.random.fold_in(own_key, axis), (), 0, length) for axis, length in enumerate(array.shape)]
        where[longest] = (where[longest] + shift) % array.shape[longest]
        spots.append(tuple(where))
    return array.at[spots[0]].set(smallest).at[spots[1]].set(largest)


def levels(stream_key, shape, cuts, least, largest):
    loudness, own = 1.0, jax.random.fold_in(stream_key, 6)
    for position, shards_of in cuts:
        heights = jnp.exp(jax.random.uniform(jax.random.fold_in(own, position), (shards_of,), jnp.float32, least / len(cuts), largest / len(cuts)))
        loudness = loudness * jnp.repeat(heights, shape[position] // shards_of).reshape([-1 if axis == position else 1 for axis in range(len(shape))])
    return loudness


def skewed_wide(own_key, dims, amount, skew):
    portions = [min(1 << octave, amount + 1 - (1 << octave)) * (1 << 20) // math.isqrt((1 << octave) ** skew) + 1 for octave in range((amount + 1).bit_length()) if 1 << octave <= amount]
    width = 1 + sum(portions) // (1 << 30)
    listing = np.cumsum(np.array([max(1, weight // width) for weight in portions]))
    pick = jax.random.randint(jax.random.fold_in(own_key, 1), dims, 0, int(listing[len(portions) - 1]))
    start = jnp.left_shift(1, jnp.searchsorted(jnp.asarray(listing, jnp.int32), pick, side="right").astype(jnp.int32))
    grade = start - 1 + jax.random.randint(jax.random.fold_in(own_key, 4), dims, 0, 1 << 30) % jnp.minimum(start, amount + 1 - start)
    return jax.random.permutation(jax.random.fold_in(own_key, 2), amount)[grade].astype(jnp.int32)


def centred(stream_key, dims, spread, limit, cuts=(), held_as=jnp.bfloat16):
    factor_of = levels(stream_key, dims, cuts, -0.22, 0.18) if cuts else 1.0
    entries = jax.random.normal(stream_key, dims, jnp.float32) * spread * factor_of
    return jnp.minimum(jnp.maximum(entries, -limit), limit).astype(held_as)


def setup_inputs(seed: int = 0) -> dict:
    arg_keys = jax.random.split(jax.random.key(seed), 7)
    return {
        "hidden": centred(arg_keys[0], (ROWS, D), 1.0, 6.0, ((0, 128),)),
        "norm_gain": jnp.clip(1.0 + 0.15 * jax.random.normal(arg_keys[1], (D,), jnp.float32), 0.25, 1.75),
        "unembed": centred(arg_keys[2], (D, V), D ** -0.5, 0.15625, ((1, 16),)),
        "verifier_logits": draw_verifier_logits(jax.random.fold_in(arg_keys[6], 71), 0),
        "served_ids": set_ends(skewed_wide(arg_keys[4], (ROWS,), V, 2), jax.random.fold_in(arg_keys[4], 3), 0, V - 1).astype(jnp.int32),
        "accepted": set_ends(jax.random.randint(arg_keys[5], (BLOCKS,), 0, DRAFT + 1), jax.random.fold_in(arg_keys[5], 1), 0, DRAFT).astype(jnp.int32),
    }


def softmax_rows(logits):
    top = lax.optimization_barrier(jnp.max(logits, axis=-1, keepdims=True))
    expo = jnp.exp(logits - top)
    return expo / lax.optimization_barrier(jnp.sum(expo, axis=-1, keepdims=True))

def reference(hidden, norm_gain, unembed, verifier_logits, served_ids, accepted):
    group = ROWS // N_DP
    slot_index = jnp.arange(ROWS, dtype=jnp.int32) % DRAFT
    block_accept = jnp.repeat(accepted, DRAFT)
    row_weight = jnp.where(slot_index <= block_accept, 1.0, 0.2).astype(jnp.float32)
    columns = jnp.arange(V, dtype=jnp.int32)

    def step(total, group_index):
        start = (group_index * group).astype(jnp.int32)
        hid_rows = lax.dynamic_slice_in_dim(hidden, start, group, 0).astype(jnp.float32)
        verif = lax.dynamic_slice_in_dim(verifier_logits, start, group, 0).astype(jnp.float32)
        row_ids = lax.dynamic_slice_in_dim(served_ids, start, group, 0)
        weights = lax.dynamic_slice_in_dim(row_weight, start, group, 0)
        inverse = lax.rsqrt(lax.optimization_barrier(jnp.mean(hid_rows * hid_rows, axis=-1, keepdims=True)) + 1e-06)
        normed = hid_rows * inverse
        scaled = (normed * norm_gain).astype(jnp.bfloat16)
        drafter = jnp.dot(scaled, unembed, preferred_element_type=jnp.float32).astype(jnp.bfloat16)
        draft_prob = softmax_rows(drafter.astype(jnp.float32))
        verif_prob = softmax_rows(verif)
        onehot = (row_ids[:, None] == columns[None, :]).astype(jnp.float32)
        target = 0.8 * verif_prob + 0.2 * onehot
        grad_logits = (weights[:, None] * (draft_prob - target)).astype(jnp.bfloat16)
        grad_normed = lax.dot_general(grad_logits, unembed, (((1,), (1,)), ((), ())), preferred_element_type=jnp.float32)
        grad_y = grad_normed * norm_gain
        inner = lax.optimization_barrier(jnp.mean(grad_y * normed, axis=-1, keepdims=True))
        grad_rows = (inverse * (grad_y - normed * inner)).astype(jnp.bfloat16)
        partial_sum = lax.dot_general(scaled, grad_logits, (((0,), (0,)), ((), ())), preferred_element_type=jnp.float32)
        partial_sum = lax.optimization_barrier(partial_sum.astype(jnp.bfloat16)).astype(jnp.float32)
        return (total + partial_sum, grad_rows)
    total, grad_parts = lax.scan(step, jnp.zeros((D, V), jnp.float32), jnp.arange(N_DP, dtype=jnp.int32))
    grad_hidden = grad_parts.reshape(ROWS, D)
    return (total.astype(jnp.bfloat16), grad_hidden)
```

```python
import functools

import jax
import jax.numpy as jnp
from jax import lax
from jax.experimental import pallas as pl
from jax.experimental.pallas import tpu as pltpu
from jax.sharding import PartitionSpec as P

DRAFT = 8
MESH = pl.DeviceIdType.MESH
F32 = jnp.float32
BF16 = jnp.bfloat16
LANES = 128
CHUNK = 256


def wait_bytes(ref, sem):
    pltpu.make_async_copy(ref, ref, sem).wait()


def to_columns(row):
    return jnp.transpose(jnp.broadcast_to(row, (LANES, LANES)))


def log_sum_rows(ref, rows, lse_ref):
    block, width = 64, ref.shape[1]

    @pl.loop(0, rows // block)
    def _(index):
        at = pl.ds(pl.multiple_of(index * block, block), block)
        tops = [ref[at, j * LANES:(j + 1) * LANES].astype(F32) for j in range(4)]
        for j in range(4, width // LANES):
            tops[j % 4] = jnp.maximum(tops[j % 4], ref[at, j * LANES:(j + 1) * LANES].astype(F32))
        top = jnp.maximum(jnp.maximum(tops[0], tops[1]), jnp.maximum(tops[2], tops[3]))
        top = jnp.max(top, axis=-1, keepdims=True)
        wide = jnp.broadcast_to(top, (block, LANES))
        sums = [jnp.zeros((block, LANES), F32) for _ in range(2)]
        for j in range(width // LANES):
            sums[j % 2] += jnp.exp(ref[at, j * LANES:(j + 1) * LANES].astype(F32) - wide)
        total = jnp.sum(sums[0] + sums[1], axis=-1, keepdims=True)
        lse_ref[at, :] = jnp.broadcast_to(top + jnp.log(total), (block, LANES))


def pack_rows(lse_ref, stat_ref, rows):
    same = lax.broadcasted_iota(jnp.int32, (LANES, LANES), 0) == lax.broadcasted_iota(jnp.int32, (LANES, LANES), 1)
    for b in range(rows // LANES):
        picked = jnp.where(same, lse_ref[b * LANES:(b + 1) * LANES, :], 0.0)
        stat_ref[0, b:b + 1, :] = jnp.sum(picked, axis=0, keepdims=True)


def combine(stat_ref):
    stats = stat_ref[...]
    top = jnp.max(stats, axis=0)
    return top + jnp.log(jnp.sum(jnp.exp(stats - top[None]), axis=0))


def kernel(n_dp, n_t, hid_ref, gain_ref, u_hbm, v_hbm, ids_ref, lw_ref, out_u, out_h,
           u_ref, v_ref, g_ref, gp_ref, sc_ref, tr_ref, ot_ref, pt_ref, p_ref, f_ref, o_ref, s_ref,
           gn_ref, gr_ref, lse_ref, a_ref, b_ref, i_ref, w_ref, vst_ref, dst_ref,
           v_sem, u_sem, ag_send, ag_recv, vs_send, vs_recv, ds_send, ds_recv, pt_send, pt_recv,
           g_send, g_recv, y_send, f_recv, o_recv, s_recv, n_send, n_recv):
    rows, width = v_ref.shape
    owned, depth = hid_ref.shape
    chunks = width // CHUNK
    part = out_u.shape[0]
    n_y = n_dp // 2
    dp, t = lax.axis_index("dp"), lax.axis_index("tensor")
    y, core = dp // 2, lax.rem(dp, 2)
    partner = (dp + 1 - 2 * core, t)
    up = (lax.rem(dp + 2, n_dp), t)
    down = (lax.rem(dp + n_dp - 2, n_dp), t)

    v_copy = pltpu.make_async_copy(v_hbm, v_ref, v_sem)
    v_copy.start()

    def columns(i):
        return pl.ds(pl.multiple_of(i * CHUNK, CHUNK), CHUNK)

    def u_copy(i):
        return pltpu.make_async_copy(u_hbm.at[:, columns(i)], u_ref.at[:, columns(i)], u_sem.at[i])

    @pl.loop(0, chunks)
    def _(i):
        u_copy(i).start()

    barrier = pltpu.get_barrier_semaphore()

    @pl.loop(1, n_t)
    def _(k):
        pl.semaphore_signal(barrier, inc=1, device_id=(dp, lax.rem(t + k, n_t)), device_id_type=MESH)

    for other in (partner, up, down):
        pl.semaphore_signal(barrier, inc=1, device_id=other, device_id_type=MESH)

    hidden = hid_ref[...].astype(F32)
    inverse = lax.rsqrt(jnp.mean(hidden * hidden, axis=-1, keepdims=True) + 1e-06)
    own = pl.ds(pl.multiple_of(t * owned, owned), owned)
    sc_ref[own, :] = (hidden * inverse * gain_ref[...]).astype(BF16)
    pl.semaphore_wait(barrier, n_t + 2)

    @pl.loop(1, n_t)
    def _(k):
        pltpu.make_async_remote_copy(
            sc_ref.at[own], sc_ref.at[own], ag_send, ag_recv,
            device_id=(dp, lax.rem(t + k, n_t)), device_id_type=MESH).start()

    v_copy.wait()
    log_sum_rows(v_ref, rows, lse_ref)
    vst_ref[0] = jnp.zeros(vst_ref.shape[1:], F32)
    dst_ref[0] = jnp.zeros(dst_ref.shape[1:], F32)
    pack_rows(lse_ref, vst_ref, rows)

    @pl.loop(1, n_t)
    def _(k):
        pltpu.make_async_remote_copy(
            vst_ref.at[0], vst_ref.at[k], vs_send, vs_recv,
            device_id=(dp, lax.rem(t + k, n_t)), device_id_type=MESH).start()

    wait_bytes(sc_ref.at[pl.ds(0, rows - owned)], ag_recv)

    @pl.loop(0, chunks)
    def _(i):
        u_copy(i).wait()
        g_ref[:, columns(i)] = jnp.dot(
            sc_ref[...], u_ref[:, columns(i)], preferred_element_type=F32).astype(BF16)

    log_sum_rows(g_ref, rows, lse_ref)
    pack_rows(lse_ref, dst_ref, rows)

    @pl.loop(1, n_t)
    def _(k):
        pltpu.make_async_remote_copy(
            dst_ref.at[0], dst_ref.at[k], ds_send, ds_recv,
            device_id=(dp, lax.rem(t + k, n_t)), device_id_type=MESH).start()

    @pl.loop(0, depth // CHUNK)
    def _(i):
        tr_ref[columns(i), :] = jnp.transpose(sc_ref[:, columns(i)])

    def pt_copy(k):
        block = pl.ds(pl.multiple_of((2 * lax.rem(y + k, n_y) + 1 - core) * part, 16), part)
        return pltpu.make_async_remote_copy(
            tr_ref.at[block], pt_ref.at[pl.ds(k * part, part)], pt_send, pt_recv,
            device_id=partner, device_id_type=MESH)

    for k in range(n_y):
        pt_copy(k).start()
    for k in range(n_y):
        block = pl.ds(pl.multiple_of((2 * lax.rem(y + k, n_y) + core) * part, 16), part)
        ot_ref[k * part:(k + 1) * part, :] = tr_ref[block, :]

    wait_bytes(vst_ref.at[pl.ds(0, n_t - 1)], vs_recv)
    wait_bytes(dst_ref.at[pl.ds(0, n_t - 1)], ds_recv)
    log_weight = lw_ref[...]
    draft_off = combine(dst_ref) - log_weight
    verif_off = combine(vst_ref) - log_weight - jnp.log(F32(0.8))
    served = 0.2 * jnp.exp(log_weight)
    for b in range(rows // LANES):
        at = slice(b * LANES, (b + 1) * LANES)
        a_ref[at, :] = to_columns(draft_off[b:b + 1])
        b_ref[at, :] = to_columns(verif_off[b:b + 1])
        w_ref[at, :] = to_columns(served[b:b + 1])
        i_ref[at, :] = to_columns(ids_ref[b:b + 1, :] - t * width)

    lane = lax.broadcasted_iota(jnp.int32, (64, LANES), 1)

    def grads(i):
        for b in range(rows // 64):
            at = slice(b * 64, (b + 1) * 64)
            for j in range(CHUNK // LANES):
                col = pl.ds(pl.multiple_of(i * CHUNK + j * LANES, LANES), LANES)
                draft = jnp.exp(g_ref[at, col].astype(F32) - a_ref[at, :])
                verif = jnp.exp(v_ref[at, col].astype(F32) - b_ref[at, :])
                hit = i_ref[at, :] - (i * CHUNK + j * LANES) == lane
                g_ref[at, col] = (draft - verif - jnp.where(hit, w_ref[at, :], 0.0)).astype(BF16)

    def g_copy(i):
        return pltpu.make_async_remote_copy(
            g_ref.at[:, columns(i)], gp_ref.at[:, columns(i)], g_send, g_recv.at[i],
            device_id=partner, device_id_type=MESH)

    def left(i):
        return pl.ds(pl.multiple_of(i * CHUNK, LANES), LANES)

    def right(i):
        return pl.ds(pl.multiple_of(i * CHUNK + LANES, LANES), LANES)

    def slab(k):
        return pl.ds(k * part, part)

    def y_copy(k, col, dst_ref, sem, to):
        return pltpu.make_async_remote_copy(
            p_ref.at[slab(k), col], dst_ref.at[:, col], y_send, sem, device_id=to, device_id_type=MESH)

    def product(i):
        p_ref[:, columns(i)] = (
            jnp.dot(ot_ref[...], g_ref[:, columns(i)], preferred_element_type=F32)
            + jnp.dot(pt_ref[...], gp_ref[:, columns(i)], preferred_element_type=F32)).astype(BF16)

    def first_sends(i):
        y_copy(2, left(i), f_ref, f_recv.at[i, 0], down).start()
        y_copy(2, right(i), f_ref, f_recv.at[i, 1], up).start()
        y_copy(1, left(i), o_ref, o_recv, up).start()
        y_copy(3, right(i), o_ref, o_recv, down).start()

    grads(0)
    g_copy(0).start()
    wait_bytes(pt_ref, pt_recv)

    @pl.loop(1, chunks)
    def _(i):
        grads(i)
        g_copy(i).start()
        g_copy(i - 1).wait_recv()
        product(i - 1)
        first_sends(i - 1)

    g_copy(chunks - 1).wait_recv()
    product(chunks - 1)
    first_sends(chunks - 1)

    @pl.loop(0, depth // CHUNK)
    def _(n):
        block = pl.ds(pl.multiple_of(n * CHUNK, CHUNK), CHUNK)
        gn_ref[:, block] = lax.dot_general(
            g_ref[...], u_ref[block, :], (((1,), (1,)), ((), ())), preferred_element_type=F32).astype(BF16)

    @pl.loop(1, n_t)
    def _(k):
        peer = lax.rem(t + k, n_t)
        pltpu.make_async_remote_copy(
            gn_ref.at[pl.ds(pl.multiple_of(peer * owned, owned), owned)], gr_ref.at[k], n_send, n_recv,
            device_id=(dp, peer), device_id_type=MESH).start()

    def add_hop(i, side):
        k, col = (3, left(i)) if side == 0 else (1, right(i))
        p_ref[slab(k), col] = (p_ref[slab(k), col].astype(F32) + f_ref[:, col].astype(F32)).astype(BF16)
        y_copy(k, col, s_ref, s_recv.at[i, side], down if side == 0 else up).start()

    @pl.loop(0, chunks)
    def _(i):
        y_copy(2, left(i), f_ref, f_recv.at[i, 0], down).wait_recv()
        add_hop(i, 0)
        y_copy(2, right(i), f_ref, f_recv.at[i, 1], up).wait_recv()
        add_hop(i, 1)

    wait_bytes(gr_ref.at[pl.ds(0, n_t - 1)], n_recv)
    grad = gn_ref[own, :].astype(F32)
    for k in range(1, n_t):
        grad += gr_ref[k].astype(F32)
    hidden = hid_ref[...].astype(F32)
    inverse = lax.rsqrt(jnp.mean(hidden * hidden, axis=-1, keepdims=True) + 1e-06)
    normed = hidden * inverse
    grad = grad * gain_ref[...]
    inner = jnp.mean(grad * normed, axis=-1, keepdims=True)
    out_h[...] = (inverse * (grad - normed * inner)).astype(BF16)

    wait_bytes(o_ref, o_recv)

    @pl.loop(0, chunks)
    def _(i):
        y_copy(3, left(i), s_ref, s_recv.at[i, 0], down).wait_recv()
        y_copy(1, right(i), s_ref, s_recv.at[i, 1], up).wait_recv()
        cols = columns(i)
        out_u[:, cols] = (
            p_ref[slab(0), cols].astype(F32) + o_ref[:, cols].astype(F32) + s_ref[:, cols].astype(F32)).astype(BF16)

    wait_bytes(sc_ref.at[pl.ds(0, rows - owned)], ag_send)
    wait_bytes(vst_ref.at[pl.ds(0, n_t - 1)], vs_send)
    wait_bytes(dst_ref.at[pl.ds(0, n_t - 1)], ds_send)
    wait_bytes(pt_ref, pt_send)
    wait_bytes(g_ref, g_send)
    wait_bytes(p_ref.at[pl.ds(0, 3 * part)], y_send)
    wait_bytes(gr_ref.at[pl.ds(0, n_t - 1)], n_send)


def body(n_dp, n_t, hidden, norm_gain, unembed, verifier_logits, served_ids, accepted):
    owned, depth = hidden.shape
    rows, width = verifier_logits.shape
    part = depth // n_dp
    chunks = width // CHUNK
    slot = jnp.arange(rows, dtype=jnp.int32) % DRAFT
    log_weight = jnp.where(slot <= jnp.repeat(accepted, DRAFT), 0.0, jnp.log(F32(0.2))).astype(F32)
    pad = ((0, 8 - rows // LANES), (0, 0))
    log_weight = jnp.pad(log_weight.reshape(rows // LANES, LANES), pad)
    ids = jnp.pad(served_ids.reshape(rows // LANES, LANES), pad)
    vmem = pl.BlockSpec(memory_space=pltpu.VMEM)
    hbm = pl.BlockSpec(memory_space=pl.ANY)
    dma = pltpu.SemaphoreType.DMA
    return pl.pallas_call(
        functools.partial(kernel, n_dp, n_t),
        out_shape=(
            jax.ShapeDtypeStruct((part, width), BF16),
            jax.ShapeDtypeStruct((owned, depth), BF16),
        ),
        in_specs=[vmem, vmem, hbm, hbm, vmem, vmem],
        out_specs=(vmem, vmem),
        scratch_shapes=[
            pltpu.VMEM((depth, width), BF16),
            pltpu.VMEM((rows, width), BF16),
            pltpu.VMEM((rows, width), BF16),
            pltpu.VMEM((rows, width), BF16),
            pltpu.VMEM((rows, depth), BF16),
            pltpu.VMEM((depth, rows), BF16),
            pltpu.VMEM((depth // 2, rows), BF16),
            pltpu.VMEM((depth // 2, rows), BF16),
            pltpu.VMEM((depth // 2, width), BF16),
            pltpu.VMEM((part, width), BF16),
            pltpu.VMEM((part, width), BF16),
            pltpu.VMEM((part, width), BF16),
            pltpu.VMEM((rows, depth), BF16),
            pltpu.VMEM((n_t, owned, depth), BF16),
            pltpu.VMEM((rows, LANES), F32),
            pltpu.VMEM((rows, LANES), F32),
            pltpu.VMEM((rows, LANES), F32),
            pltpu.VMEM((rows, LANES), jnp.int32),
            pltpu.VMEM((rows, LANES), F32),
            pltpu.VMEM((n_t, 8, LANES), F32),
            pltpu.VMEM((n_t, 8, LANES), F32),
            dma, dma((chunks,)), dma, dma, dma, dma, dma, dma, dma, dma,
            dma, dma((chunks,)), dma, dma((chunks, 2)), dma, dma((chunks, 2)), dma, dma,
        ],
        compiler_params=pltpu.CompilerParams(
            collective_id=0, has_side_effects=True, vmem_limit_bytes=62 * 1024 * 1024),
        cost_estimate=pl.CostEstimate(
            flops=6 * rows * depth * width, bytes_accessed=2 * (depth + rows + part) * width,
            transcendentals=4 * rows * width),
    )(hidden, norm_gain.reshape(1, depth), unembed, verifier_logits, ids, log_weight)


def solution(mesh):
    n_dp, n_t = mesh.shape["dp"], mesh.shape["tensor"]

    def run(*args):
        return body(n_dp, n_t, *args)

    return jax.shard_map(
        run,
        mesh=mesh,
        in_specs=(
            P(("dp", "tensor"), None),
            P(),
            P(None, "tensor"),
            P("dp", "tensor"),
            P("dp"),
            P("dp"),
        ),
        out_specs=(P("dp", "tensor"), P(("dp", "tensor"), None)),
        check_vma=False,
    )
```

```python
import functools

import jax
import jax.numpy as jnp
from jax import lax
from jax.experimental import pallas as pl
from jax.experimental.pallas import tpu as pltpu
from jax.sharding import PartitionSpec as P

DRAFT = 8
SIDE = 4
LOG_LOW = -1.6094379124341003
MESH = pl.DeviceIdType.MESH
F32 = jnp.float32
BF16 = jnp.bfloat16
LANES = 128
CHUNK = 256


def wait_bytes(ref, sem):
    pltpu.make_async_copy(ref, ref, sem).wait()


def to_columns(row):
    return jnp.transpose(jnp.broadcast_to(row, (LANES, LANES)))


def log_sum_rows(ref, index, lse_ref):
    block, width = 32, ref.shape[1]
    at = pl.ds(pl.multiple_of(index * block, block), block)
    tops = [ref[at, j * LANES:(j + 1) * LANES].astype(F32) for j in range(2)]
    for j in range(2, width // LANES):
        tops[j % 2] = jnp.maximum(tops[j % 2], ref[at, j * LANES:(j + 1) * LANES].astype(F32))
    top = jnp.max(jnp.maximum(tops[0], tops[1]), axis=-1, keepdims=True)
    wide = jnp.broadcast_to(top, (block, LANES))
    sums = [jnp.zeros((block, LANES), F32) for _ in range(2)]
    for j in range(width // LANES):
        sums[j % 2] += jnp.exp(ref[at, j * LANES:(j + 1) * LANES].astype(F32) - wide)
    total = jnp.sum(sums[0] + sums[1], axis=-1, keepdims=True)
    lse_ref[at, :] = jnp.broadcast_to(top + jnp.log(total), (block, LANES))


def pack_rows(lse_ref, stat_ref, rows):
    same = lax.broadcasted_iota(jnp.int32, (LANES, LANES), 0) == lax.broadcasted_iota(jnp.int32, (LANES, LANES), 1)
    for b in range(rows // LANES):
        picked = jnp.where(same, lse_ref[b * LANES:(b + 1) * LANES, :], 0.0)
        stat_ref[0, b:b + 1, :] = jnp.sum(picked, axis=0, keepdims=True)


def combine(stat_ref):
    stats = stat_ref[...]
    top = jnp.max(stats, axis=0)
    return top + jnp.log(jnp.sum(jnp.exp(stats - top[None]), axis=0))


def kernel(n_dp, n_t, hid_ref, gain_ref, u_hbm, v_hbm, ids_ref, acc_ref, out_u, out_h,
           u_ref, v_ref, g_ref, gp_ref, sc_ref, tr_ref, ot_ref, pt_ref, p_ref, f_ref, o_ref, s_ref,
           gn_ref, gr_ref, lse_ref, a_ref, b_ref, i_ref, w_ref, lw_ref, m_ref, z_ref, vst_ref, dst_ref,
           v_sem, u_sem, ag_send, r1_sem, r2_sem, r3_sem, vs_send, vs_recv, ds_send, ds_recv, pt_send, pt_recv,
           g_send, g_recv, y_send, f_recv, o_recv, s_recv, n_send, n_recv):
    rows, width = v_ref.shape
    owned, depth = hid_ref.shape
    chunks = width // CHUNK
    part = out_u.shape[0]
    n_y = n_dp // 2
    dp, t = lax.axis_index("dp"), lax.axis_index("tensor")
    y, core = dp // 2, lax.rem(dp, 2)
    partner = (dp + 1 - 2 * core, t)
    up = (lax.rem(dp + 2, n_dp), t)
    down = (lax.rem(dp + n_dp - 2, n_dp), t)

    v_copy = pltpu.make_async_copy(v_hbm, v_ref, v_sem)
    v_copy.start()

    def columns(i):
        return pl.ds(pl.multiple_of(i * CHUNK, CHUNK), CHUNK)

    def u_copy(i):
        return pltpu.make_async_copy(u_hbm.at[:, columns(i)], u_ref.at[:, columns(i)], u_sem.at[i])

    @pl.loop(0, chunks)
    def _(i):
        u_copy(i).start()

    barrier = pltpu.get_barrier_semaphore()

    @pl.loop(1, n_t)
    def _(k):
        pl.semaphore_signal(barrier, inc=1, device_id=(dp, lax.rem(t + k, n_t)), device_id_type=MESH)

    for other in (partner, up, down):
        pl.semaphore_signal(barrier, inc=1, device_id=other, device_id_type=MESH)

    z, x = t // SIDE, lax.rem(t, SIDE)
    place = (x, z)

    def first_axis(half, off):
        if half == 0:
            return (dp, z * SIDE + lax.rem(x + off, SIDE))
        return (dp, lax.rem(z + off, SIDE) * SIDE + x)

    def second_axis(half, off):
        return first_axis(1 - half, off)

    def line_copy(half, off):
        block = sc_ref.at[0, half, place[half]]
        return pltpu.make_async_remote_copy(
            block, block, ag_send, r1_sem.at[half, off],
            device_id=first_axis(half, off), device_id_type=MESH)

    def cross_copy(half, off, back):
        o = lax.rem(place[half] + SIDE - off, SIDE)
        return pltpu.make_async_remote_copy(
            sc_ref.at[0, half, o], sc_ref.at[1 if back else 2, half, o], ag_send, r2_sem.at[half, off, back],
            device_id=second_axis(half, SIDE - 1 if back else 1), device_id_type=MESH)

    def relay_copy(half, off, back):
        o = lax.rem(place[half] + SIDE - off, SIDE)
        cols = pl.ds(depth // 2, depth // 2) if back else pl.ds(0, depth // 2)
        return pltpu.make_async_remote_copy(
            sc_ref.at[1 if back else 2, half, o, :, cols], sc_ref.at[3, half, o, :, cols], ag_send, r3_sem,
            device_id=second_axis(half, SIDE - 1 if back else 1), device_id_type=MESH)

    hidden = hid_ref[...].astype(F32)
    inverse = lax.rsqrt(jnp.mean(hidden * hidden, axis=-1, keepdims=True) + 1e-06)
    scaled = (hidden * inverse * gain_ref[...][None, :]).astype(BF16)
    for half in range(2):
        sc_ref[0, half, place[half]] = scaled[half * owned // 2:(half + 1) * owned // 2]
    pl.semaphore_wait(barrier, n_t + 2)

    for off in (1, 3, 2):
        for half in range(2):
            line_copy(half, off).start()
    for half in range(2):
        for back in range(2):
            cross_copy(half, 0, back).start()

    m_ref[...] = jnp.full(m_ref.shape, -jnp.inf, F32)
    z_ref[...] = jnp.zeros(z_ref.shape, F32)
    vst_ref[0] = jnp.zeros(vst_ref.shape[1:], F32)
    dst_ref[0] = jnp.zeros(dst_ref.shape[1:], F32)
    blocks = rows // DRAFT
    for b in range(rows // LANES):
        at = slice(b * LANES, (b + 1) * LANES)
        row = b * LANES + lax.broadcasted_iota(jnp.int32, (LANES, blocks), 0)
        same = lax.shift_right_logical(row, 3) == lax.broadcasted_iota(jnp.int32, (LANES, blocks), 1)
        count = jnp.sum(jnp.where(same, acc_ref[...].astype(F32), 0.0), axis=-1, keepdims=True)
        slot = (lax.broadcasted_iota(jnp.int32, (LANES, LANES), 0) & (DRAFT - 1)).astype(F32)
        kept = slot <= jnp.broadcast_to(count, (LANES, LANES))
        lw_ref[at, :] = jnp.where(kept, 0.0, LOG_LOW)
        w_ref[at, :] = jnp.where(kept, 0.2, 0.2 * 0.2)
        i_ref[at, :] = to_columns(ids_ref[b:b + 1, :] - t * width)

    def forward_cross(off):
        for half in range(2):
            line_copy(half, off).wait_recv()
            for back in range(2):
                cross_copy(half, off, back).start()

    def forward_relay(off):
        for half in range(2):
            for back in range(2):
                cross_copy(half, off, back).wait_recv()
                relay_copy(half, off, back).start()

    forward_cross(1)
    forward_cross(3)
    forward_relay(0)
    forward_cross(2)
    for off in (1, 3, 2):
        forward_relay(off)
    v_copy.wait()

    quarter = rows // SIDE

    def home(block):
        slot, half, o = block // 8, block // 4 % 2, block % 4
        far = lax.rem(place[1 - half] + (0, 1, SIDE - 1, 2)[slot], SIDE)
        if half == 0:
            return pl.multiple_of(far * quarter + o * owned, 16)
        return pl.multiple_of(o * quarter + far * owned + 16, 16)

    def drafter(i, lo, hi):
        count = (hi - lo) * quarter
        logits = jnp.dot(
            sc_ref[lo:hi].reshape(count, depth), u_ref[:, columns(i)], preferred_element_type=F32).astype(BF16)
        for b in range(count // 16):
            g_ref[pl.ds(home(lo * 8 + b), 16), columns(i)] = logits[b * 16:(b + 1) * 16]
        for b in range(count // 32):
            at = slice(lo * quarter + b * 32, lo * quarter + (b + 1) * 32)
            piece = logits[b * 32:(b + 1) * 32].astype(F32)
            tiles = [piece[:, j * LANES:(j + 1) * LANES] for j in range(CHUNK // LANES)]
            old = m_ref[at, :]
            top = old
            for tile in tiles:
                top = jnp.maximum(top, tile)
            total = z_ref[at, :] * jnp.exp(old - top)
            for tile in tiles:
                total += jnp.exp(tile - top)
            m_ref[at, :] = top
            z_ref[at, :] = total

    @pl.loop(0, chunks)
    def _(i):
        u_copy(i).wait()
        drafter(i, 0, 3)
        log_sum_rows(v_ref, jnp.minimum(i, rows // 32 - 1), lse_ref)

    pack_rows(lse_ref, vst_ref, rows)

    @pl.loop(1, n_t)
    def _(k):
        pltpu.make_async_remote_copy(
            vst_ref.at[0], vst_ref.at[k], vs_send, vs_recv,
            device_id=(dp, lax.rem(t + k, n_t)), device_id_type=MESH).start()

    wait_bytes(sc_ref.at[3], r3_sem)

    @pl.loop(0, chunks)
    def _(i):
        drafter(i, 3, 4)

    for b in range(rows // 16):
        at = slice(b * 16, (b + 1) * 16)
        top = jnp.max(m_ref[at, :], axis=-1, keepdims=True)
        total = jnp.sum(z_ref[at, :] * jnp.exp(m_ref[at, :] - top), axis=-1, keepdims=True)
        lse_ref[pl.ds(home(b), 16), :] = jnp.broadcast_to(top + jnp.log(total), (16, LANES))
    pack_rows(lse_ref, dst_ref, rows)

    @pl.loop(1, n_t)
    def _(k):
        pltpu.make_async_remote_copy(
            dst_ref.at[0], dst_ref.at[k], ds_send, ds_recv,
            device_id=(dp, lax.rem(t + k, n_t)), device_id_type=MESH).start()

    for b in range(rows // 16):
        gn_ref[pl.ds(home(b), 16), :] = sc_ref[b // 8, b // 4 % 2, b % 4]

    @pl.loop(0, depth // CHUNK)
    def _(i):
        tr_ref[columns(i), :] = jnp.transpose(gn_ref[:, columns(i)])

    def pt_copy(k):
        block = pl.ds(pl.multiple_of((2 * lax.rem(y + k, n_y) + 1 - core) * part, 16), part)
        return pltpu.make_async_remote_copy(
            tr_ref.at[block], pt_ref.at[pl.ds(k * part, part)], pt_send, pt_recv,
            device_id=partner, device_id_type=MESH)

    for k in range(n_y):
        pt_copy(k).start()
    for k in range(n_y):
        block = pl.ds(pl.multiple_of((2 * lax.rem(y + k, n_y) + core) * part, 16), part)
        ot_ref[k * part:(k + 1) * part, :] = tr_ref[block, :]

    wait_bytes(vst_ref.at[pl.ds(0, n_t - 1)], vs_recv)
    verif_off = combine(vst_ref) - jnp.log(F32(0.8))
    for b in range(rows // LANES):
        at = slice(b * LANES, (b + 1) * LANES)
        b_ref[at, :] = to_columns(verif_off[b:b + 1]) - lw_ref[at, :]
    wait_bytes(dst_ref.at[pl.ds(0, n_t - 1)], ds_recv)
    draft_off = combine(dst_ref)
    for b in range(rows // LANES):
        at = slice(b * LANES, (b + 1) * LANES)
        a_ref[at, :] = to_columns(draft_off[b:b + 1]) - lw_ref[at, :]

    lane = lax.broadcasted_iota(jnp.int32, (64, LANES), 1)

    def grads(i):
        for b in range(rows // 64):
            at = slice(b * 64, (b + 1) * 64)
            for j in range(CHUNK // LANES):
                col = pl.ds(pl.multiple_of(i * CHUNK + j * LANES, LANES), LANES)
                draft = jnp.exp(g_ref[at, col].astype(F32) - a_ref[at, :])
                verif = jnp.exp(v_ref[at, col].astype(F32) - b_ref[at, :])
                hit = i_ref[at, :] - (i * CHUNK + j * LANES) == lane
                g_ref[at, col] = (draft - verif - jnp.where(hit, w_ref[at, :], 0.0)).astype(BF16)

    def g_copy(i):
        return pltpu.make_async_remote_copy(
            g_ref.at[:, columns(i)], gp_ref.at[:, columns(i)], g_send, g_recv.at[i],
            device_id=partner, device_id_type=MESH)

    def left(i):
        return pl.ds(pl.multiple_of(i * CHUNK, LANES), LANES)

    def right(i):
        return pl.ds(pl.multiple_of(i * CHUNK + LANES, LANES), LANES)

    def slab(k):
        return pl.ds(k * part, part)

    def y_copy(k, col, dst_ref, sem, to):
        return pltpu.make_async_remote_copy(
            p_ref.at[slab(k), col], dst_ref.at[:, col], y_send, sem, device_id=to, device_id_type=MESH)

    def product(i):
        p_ref[:, columns(i)] = (
            jnp.dot(ot_ref[...], g_ref[:, columns(i)], preferred_element_type=F32)
            + jnp.dot(pt_ref[...], gp_ref[:, columns(i)], preferred_element_type=F32)).astype(BF16)

    def first_sends(i):
        y_copy(2, left(i), f_ref, f_recv.at[i, 0], down).start()
        y_copy(2, right(i), f_ref, f_recv.at[i, 1], up).start()
        y_copy(1, left(i), o_ref, o_recv, up).start()
        y_copy(3, right(i), o_ref, o_recv, down).start()

    grads(0)
    g_copy(0).start()
    wait_bytes(pt_ref, pt_recv)

    @pl.loop(1, chunks)
    def _(i):
        grads(i)
        g_copy(i).start()
        g_copy(i - 1).wait_recv()
        product(i - 1)
        first_sends(i - 1)

    g_copy(chunks - 1).wait_recv()
    product(chunks - 1)
    first_sends(chunks - 1)

    @pl.loop(0, depth // CHUNK)
    def _(n):
        block = pl.ds(pl.multiple_of(n * CHUNK, CHUNK), CHUNK)
        gn_ref[:, block] = lax.dot_general(
            g_ref[...], u_ref[block, :], (((1,), (1,)), ((), ())), preferred_element_type=F32).astype(BF16)

    @pl.loop(1, n_t)
    def _(k):
        peer = lax.rem(t + k, n_t)
        pltpu.make_async_remote_copy(
            gn_ref.at[pl.ds(pl.multiple_of(peer * owned, owned), owned)], gr_ref.at[k], n_send, n_recv,
            device_id=(dp, peer), device_id_type=MESH).start()

    def add_hop(i, side):
        k, col = (3, left(i)) if side == 0 else (1, right(i))
        p_ref[slab(k), col] = (p_ref[slab(k), col].astype(F32) + f_ref[:, col].astype(F32)).astype(BF16)
        y_copy(k, col, s_ref, s_recv.at[i, side], down if side == 0 else up).start()

    @pl.loop(0, chunks)
    def _(i):
        y_copy(2, left(i), f_ref, f_recv.at[i, 0], down).wait_recv()
        add_hop(i, 0)
        y_copy(2, right(i), f_ref, f_recv.at[i, 1], up).wait_recv()
        add_hop(i, 1)

    wait_bytes(gr_ref.at[pl.ds(0, n_t - 1)], n_recv)
    own = pl.ds(pl.multiple_of(t * owned, owned), owned)
    grad = gn_ref[own, :].astype(F32)
    for k in range(1, n_t):
        grad += gr_ref[k].astype(F32)
    hidden = hid_ref[...].astype(F32)
    inverse = lax.rsqrt(jnp.mean(hidden * hidden, axis=-1, keepdims=True) + 1e-06)
    normed = hidden * inverse
    grad = grad * gain_ref[...][None, :]
    inner = jnp.mean(grad * normed, axis=-1, keepdims=True)
    out_h[...] = (inverse * (grad - normed * inner)).astype(BF16)

    wait_bytes(o_ref, o_recv)

    @pl.loop(0, chunks)
    def _(i):
        y_copy(3, left(i), s_ref, s_recv.at[i, 0], down).wait_recv()
        y_copy(1, right(i), s_ref, s_recv.at[i, 1], up).wait_recv()
        cols = columns(i)
        out_u[:, cols] = (
            p_ref[slab(0), cols].astype(F32) + o_ref[:, cols].astype(F32) + s_ref[:, cols].astype(F32)).astype(BF16)

    for part_sent in (sc_ref.at[0], sc_ref.at[0], sc_ref.at[3], sc_ref.at[0, 0, pl.ds(0, 3)], sc_ref.at[0, 0, pl.ds(0, 3)]):
        wait_bytes(part_sent, ag_send)
    wait_bytes(vst_ref.at[pl.ds(0, n_t - 1)], vs_send)
    wait_bytes(dst_ref.at[pl.ds(0, n_t - 1)], ds_send)
    wait_bytes(pt_ref, pt_send)
    wait_bytes(g_ref, g_send)
    wait_bytes(p_ref.at[pl.ds(0, 3 * part)], y_send)
    wait_bytes(gr_ref.at[pl.ds(0, n_t - 1)], n_send)


def body(n_dp, n_t, hidden, norm_gain, unembed, verifier_logits, served_ids, accepted):
    owned, depth = hidden.shape
    rows, width = verifier_logits.shape
    part = depth // n_dp
    chunks = width // CHUNK
    vmem = pl.BlockSpec(memory_space=pltpu.VMEM)
    hbm = pl.BlockSpec(memory_space=pl.ANY)
    dma = pltpu.SemaphoreType.DMA
    return pl.pallas_call(
        functools.partial(kernel, n_dp, n_t),
        out_shape=(
            jax.ShapeDtypeStruct((part, width), BF16),
            jax.ShapeDtypeStruct((owned, depth), BF16),
        ),
        in_specs=[vmem, vmem, hbm, hbm, vmem, vmem],
        out_specs=(vmem, vmem),
        scratch_shapes=[
            pltpu.VMEM((depth, width), BF16),
            pltpu.VMEM((rows, width), BF16),
            pltpu.VMEM((rows, width), BF16),
            pltpu.VMEM((rows, width), BF16),
            pltpu.VMEM((SIDE, 2, SIDE, owned // 2, depth), BF16),
            pltpu.VMEM((depth, rows), BF16),
            pltpu.VMEM((depth // 2, rows), BF16),
            pltpu.VMEM((depth // 2, rows), BF16),
            pltpu.VMEM((depth // 2, width), BF16),
            pltpu.VMEM((part, width), BF16),
            pltpu.VMEM((part, width), BF16),
            pltpu.VMEM((part, width), BF16),
            pltpu.VMEM((rows, depth), BF16),
            pltpu.VMEM((n_t, owned, depth), BF16),
            pltpu.VMEM((rows, LANES), F32),
            pltpu.VMEM((rows, LANES), F32),
            pltpu.VMEM((rows, LANES), F32),
            pltpu.VMEM((rows, LANES), jnp.int32),
            pltpu.VMEM((rows, LANES), F32),
            pltpu.VMEM((rows, LANES), F32),
            pltpu.VMEM((rows, LANES), F32),
            pltpu.VMEM((rows, LANES), F32),
            pltpu.VMEM((n_t, 8, LANES), F32),
            pltpu.VMEM((n_t, 8, LANES), F32),
            dma, dma((chunks,)), dma, dma((2, SIDE)), dma((2, SIDE, 2)), dma, dma, dma, dma, dma, dma, dma,
            dma, dma((chunks,)), dma, dma((chunks, 2)), dma, dma((chunks, 2)), dma, dma,
        ],
        compiler_params=pltpu.CompilerParams(
            collective_id=0, has_side_effects=True, vmem_limit_bytes=62 * 1024 * 1024),
        cost_estimate=pl.CostEstimate(
            flops=6 * rows * depth * width, bytes_accessed=2 * (depth + rows + part) * width,
            transcendentals=4 * rows * width),
    )(hidden, norm_gain, unembed, verifier_logits, served_ids.reshape(rows // LANES, LANES), accepted.reshape(1, rows // DRAFT))


def solution(mesh):
    n_dp, n_t = mesh.shape["dp"], mesh.shape["tensor"]

    def run(*args):
        return body(n_dp, n_t, *args)

    return jax.shard_map(
        run,
        mesh=mesh,
        in_specs=(
            P(("dp", "tensor"), None),
            P(),
            P(None, "tensor"),
            P("dp", "tensor"),
            P("dp"),
            P("dp"),
        ),
        out_specs=(P("dp", "tensor"), P(("dp", "tensor"), None)),
        check_vma=False,
    )
```

```python
import functools

import jax
import jax.numpy as jnp
from jax import lax
from jax.experimental import pallas as pl
from jax.experimental.pallas import tpu as pltpu
from jax.sharding import PartitionSpec as P

DRAFT = 8
SIDE = 4
WAVES = 1
LOG_LOW = -1.6094379124341003
MESH = pl.DeviceIdType.MESH
F32 = jnp.float32
BF16 = jnp.bfloat16
LANES = 128
CHUNK = 256


def wait_bytes(ref, sem):
    pltpu.make_async_copy(ref, ref, sem).wait()


def to_columns(row):
    return jnp.transpose(jnp.broadcast_to(row, (LANES, LANES)))


def log_sum_rows(ref, index, lse_ref):
    block, width = 32, ref.shape[1]
    at = pl.ds(pl.multiple_of(index * block, block), block)
    tops = [ref[at, j * LANES:(j + 1) * LANES].astype(F32) for j in range(2)]
    for j in range(2, width // LANES):
        tops[j % 2] = jnp.maximum(tops[j % 2], ref[at, j * LANES:(j + 1) * LANES].astype(F32))
    top = jnp.max(jnp.maximum(tops[0], tops[1]), axis=-1, keepdims=True)
    wide = jnp.broadcast_to(top, (block, LANES))
    sums = [jnp.zeros((block, LANES), F32) for _ in range(2)]
    for j in range(width // LANES):
        sums[j % 2] += jnp.exp(ref[at, j * LANES:(j + 1) * LANES].astype(F32) - wide)
    total = jnp.sum(sums[0] + sums[1], axis=-1, keepdims=True)
    lse_ref[at, :] = jnp.broadcast_to(top + jnp.log(total), (block, LANES))


def pack_rows(lse_ref, stat_ref, rows):
    same = lax.broadcasted_iota(jnp.int32, (LANES, LANES), 0) == lax.broadcasted_iota(jnp.int32, (LANES, LANES), 1)
    for b in range(rows // LANES):
        picked = jnp.where(same, lse_ref[b * LANES:(b + 1) * LANES, :], 0.0)
        stat_ref[0, b:b + 1, :] = jnp.sum(picked, axis=0, keepdims=True)


def combine(stat_ref):
    stats = stat_ref[...]
    top = jnp.max(stats, axis=0)
    return top + jnp.log(jnp.sum(jnp.exp(stats - top[None]), axis=0))


def kernel(n_dp, n_t, hid_ref, gain_ref, u_hbm, v_hbm, ids_ref, acc_ref, out_a, out_s, out_h,
           even_ref, odd_ref, u_ref, v_ref, g_ref, gp_ref, sc_ref, tr_ref, ot_ref, pt_ref, p_ref, f_ref, o_ref,
           gn_ref, gr_ref, lse_ref, a_ref, b_ref, i_ref, w_ref, lw_ref, m_ref, z_ref, vst_ref, dst_ref,
           v_sem, u_sem, ag_send, r1_sem, r2_sem, r3_sem, vs_send, vs_recv, ds_send, ds_recv, pt_send, pt_recv,
           g_send, g_recv, y_send, f_recv, o_recv, s_recv, a_sem, n_send, n_recv):
    rows, width = v_ref.shape
    owned, depth = hid_ref.shape
    chunks = width // CHUNK
    part = out_a.shape[0]
    n_y = n_dp // 2
    dp, t = lax.axis_index("dp"), lax.axis_index("tensor")
    y, core = dp // 2, lax.rem(dp, 2)
    partner = (dp + 1 - 2 * core, t)
    up = (lax.rem(dp + 2, n_dp), t)
    down = (lax.rem(dp + n_dp - 2, n_dp), t)

    v_copy = pltpu.make_async_copy(v_hbm, v_ref, v_sem)
    v_copy.start()

    def columns(i):
        return pl.ds(pl.multiple_of(i * CHUNK, CHUNK), CHUNK)

    def u_copy(i):
        return pltpu.make_async_copy(u_hbm.at[:, columns(i)], u_ref.at[:, columns(i)], u_sem.at[i])

    @pl.loop(0, chunks)
    def _(i):
        u_copy(i).start()

    barrier = pltpu.get_barrier_semaphore()

    @pl.loop(1, n_t)
    def _(k):
        pl.semaphore_signal(barrier, inc=1, device_id=(dp, lax.rem(t + k, n_t)), device_id_type=MESH)

    for other in (partner, up, down):
        pl.semaphore_signal(barrier, inc=1, device_id=other, device_id_type=MESH)

    z, x = t // SIDE, lax.rem(t, SIDE)
    place = (x, z)

    def first_axis(half, off):
        if half == 0:
            return (dp, z * SIDE + lax.rem(x + off, SIDE))
        return (dp, lax.rem(z + off, SIDE) * SIDE + x)

    def second_axis(half, off):
        return first_axis(1 - half, off)

    span = depth // WAVES

    def line_copy(w, half, off):
        block = sc_ref.at[0, half, place[half], :, pl.ds(w * span, span)]
        return pltpu.make_async_remote_copy(
            block, block, ag_send, r1_sem.at[w, half, off],
            device_id=first_axis(half, off), device_id_type=MESH)

    def cross_copy(w, half, off, back):
        o = lax.rem(place[half] + SIDE - off, SIDE)
        cols = pl.ds(w * span, span)
        return pltpu.make_async_remote_copy(
            sc_ref.at[0, half, o, :, cols], sc_ref.at[1 if back else 2, half, o, :, cols],
            ag_send, r2_sem.at[w, half, off, back],
            device_id=second_axis(half, SIDE - 1 if back else 1), device_id_type=MESH)

    def relay_copy(w, half, off, back):
        o = lax.rem(place[half] + SIDE - off, SIDE)
        cols = pl.ds(w * span + back * span // 2, span // 2)
        return pltpu.make_async_remote_copy(
            sc_ref.at[1 if back else 2, half, o, :, cols], sc_ref.at[3, half, o, :, cols], ag_send, r3_sem.at[w],
            device_id=second_axis(half, SIDE - 1 if back else 1), device_id_type=MESH)

    def begin(w):
        for off in (1, 3, 2):
            for half in range(2):
                line_copy(w, half, off).start()
        for half in range(2):
            for back in range(2):
                cross_copy(w, half, 0, back).start()

    def forward_cross(w, off):
        for half in range(2):
            line_copy(w, half, off).wait_recv()
            for back in range(2):
                cross_copy(w, half, off, back).start()

    def forward_relay(w, off):
        for half in range(2):
            for back in range(2):
                cross_copy(w, half, off, back).wait_recv()
                relay_copy(w, half, off, back).start()

    def gathered(w):
        wait_bytes(sc_ref.at[3, :, :, :, pl.ds(w * span, span)], r3_sem.at[w])

    def verifier(first, last):
        @pl.loop(first, last)
        def _(i):
            log_sum_rows(v_ref, i, lse_ref)

    hidden = hid_ref[...].astype(F32)
    inverse = lax.rsqrt(jnp.mean(hidden * hidden, axis=-1, keepdims=True) + 1e-06)
    scaled = (hidden * inverse * gain_ref[...][None, :]).astype(BF16)
    for half in range(2):
        sc_ref[0, half, place[half]] = scaled[half * owned // 2:(half + 1) * owned // 2]
    pl.semaphore_wait(barrier, n_t + 2)

    begin(0)
    m_ref[...] = jnp.full(m_ref.shape, -jnp.inf, F32)
    z_ref[...] = jnp.zeros(z_ref.shape, F32)
    vst_ref[0] = jnp.zeros(vst_ref.shape[1:], F32)
    dst_ref[0] = jnp.zeros(dst_ref.shape[1:], F32)
    blocks = rows // DRAFT
    for b in range(rows // LANES):
        at = slice(b * LANES, (b + 1) * LANES)
        row = b * LANES + lax.broadcasted_iota(jnp.int32, (LANES, blocks), 0)
        same = lax.shift_right_logical(row, 3) == lax.broadcasted_iota(jnp.int32, (LANES, blocks), 1)
        count = jnp.sum(jnp.where(same, acc_ref[...].astype(F32), 0.0), axis=-1, keepdims=True)
        slot = (lax.broadcasted_iota(jnp.int32, (LANES, LANES), 0) & (DRAFT - 1)).astype(F32)
        kept = slot <= jnp.broadcast_to(count, (LANES, LANES))
        lw_ref[at, :] = jnp.where(kept, 0.0, LOG_LOW)
        w_ref[at, :] = jnp.where(kept, 0.2, 0.2 * 0.2)
        i_ref[at, :] = to_columns(ids_ref[b:b + 1, :] - t * width)

    v_copy.wait()
    forward_cross(0, 1)
    forward_cross(0, 3)
    verifier(0, 3)
    forward_relay(0, 0)
    verifier(3, 6)
    forward_cross(0, 2)
    verifier(6, 9)
    forward_relay(0, 1)
    verifier(9, 11)
    forward_relay(0, 3)
    verifier(11, 13)
    forward_relay(0, 2)
    verifier(13, rows // 32)
    pack_rows(lse_ref, vst_ref, rows)

    @pl.loop(1, n_t)
    def _(k):
        pltpu.make_async_remote_copy(
            vst_ref.at[0], vst_ref.at[k], vs_send, vs_recv,
            device_id=(dp, lax.rem(t + k, n_t)), device_id_type=MESH).start()

    gathered(0)

    @pl.loop(0, chunks)
    def _(i):
        u_copy(i).wait()

    quarter = rows // SIDE

    def home(block):
        slot, half, o = block // 8, block // 4 % 2, block % 4
        far = lax.rem(place[1 - half] + (0, 1, SIDE - 1, 2)[slot], SIDE)
        if half == 0:
            return pl.multiple_of(far * quarter + o * owned, 16)
        return pl.multiple_of(o * quarter + far * owned + 16, 16)

    def drafter(i, buf):
        buf[...] = jnp.dot(sc_ref[...].reshape(rows, depth), u_ref[:, columns(i)], preferred_element_type=F32)

    def gather_stats(i, buf):
        for b in range(rows // 32):
            at = slice(b * 32, (b + 1) * 32)
            logits = buf[at, :].astype(BF16)
            for h in range(2):
                g_ref[pl.ds(home(2 * b + h), 16), columns(i)] = logits[h * 16:(h + 1) * 16]
            piece = logits.astype(F32)
            tiles = [piece[:, j * LANES:(j + 1) * LANES] for j in range(CHUNK // LANES)]
            old = m_ref[at, :]
            top = old
            for tile in tiles:
                top = jnp.maximum(top, tile)
            total = z_ref[at, :] * jnp.exp(old - top)
            for tile in tiles:
                total += jnp.exp(tile - top)
            m_ref[at, :] = top
            z_ref[at, :] = total

    drafter(0, even_ref)

    @pl.loop(0, chunks // 2)
    def _(j):
        drafter(2 * j + 1, odd_ref)
        gather_stats(2 * j, even_ref)
        drafter(2 * j + 2, even_ref)
        gather_stats(2 * j + 1, odd_ref)

    gather_stats(chunks - 1, even_ref)

    for b in range(rows // 16):
        at = slice(b * 16, (b + 1) * 16)
        top = jnp.max(m_ref[at, :], axis=-1, keepdims=True)
        total = jnp.sum(z_ref[at, :] * jnp.exp(m_ref[at, :] - top), axis=-1, keepdims=True)
        lse_ref[pl.ds(home(b), 16), :] = jnp.broadcast_to(top + jnp.log(total), (16, LANES))
    pack_rows(lse_ref, dst_ref, rows)

    @pl.loop(1, n_t)
    def _(k):
        pltpu.make_async_remote_copy(
            dst_ref.at[0], dst_ref.at[k], ds_send, ds_recv,
            device_id=(dp, lax.rem(t + k, n_t)), device_id_type=MESH).start()

    for b in range(rows // 16):
        gn_ref[pl.ds(home(b), 16), :] = sc_ref[b // 8, b // 4 % 2, b % 4]

    @pl.loop(0, depth // CHUNK)
    def _(i):
        tr_ref[columns(i), :] = jnp.transpose(gn_ref[:, columns(i)])

    def pt_copy(k):
        block = pl.ds(pl.multiple_of((2 * lax.rem(y + k, n_y) + 1 - core) * part, 16), part)
        return pltpu.make_async_remote_copy(
            tr_ref.at[block], pt_ref.at[pl.ds(k * part, part)], pt_send, pt_recv,
            device_id=partner, device_id_type=MESH)

    for k in range(n_y):
        pt_copy(k).start()
    for k in range(n_y):
        block = pl.ds(pl.multiple_of((2 * lax.rem(y + k, n_y) + core) * part, 16), part)
        ot_ref[k * part:(k + 1) * part, :] = tr_ref[block, :]

    wait_bytes(vst_ref.at[pl.ds(0, n_t - 1)], vs_recv)
    verif_off = combine(vst_ref) - jnp.log(F32(0.8))
    for b in range(rows // LANES):
        at = slice(b * LANES, (b + 1) * LANES)
        b_ref[at, :] = to_columns(verif_off[b:b + 1]) - lw_ref[at, :]
    wait_bytes(dst_ref.at[pl.ds(0, n_t - 1)], ds_recv)
    draft_off = combine(dst_ref)
    for b in range(rows // LANES):
        at = slice(b * LANES, (b + 1) * LANES)
        a_ref[at, :] = to_columns(draft_off[b:b + 1]) - lw_ref[at, :]

    lane = lax.broadcasted_iota(jnp.int32, (64, LANES), 1)

    def grads(i):
        for b in range(rows // 64):
            at = slice(b * 64, (b + 1) * 64)
            for j in range(CHUNK // LANES):
                col = pl.ds(pl.multiple_of(i * CHUNK + j * LANES, LANES), LANES)
                draft = jnp.exp(g_ref[at, col].astype(F32) - a_ref[at, :])
                verif = jnp.exp(v_ref[at, col].astype(F32) - b_ref[at, :])
                hit = i_ref[at, :] - (i * CHUNK + j * LANES) == lane
                g_ref[at, col] = (draft - verif - jnp.where(hit, w_ref[at, :], 0.0)).astype(BF16)

    def g_copy(i):
        return pltpu.make_async_remote_copy(
            g_ref.at[:, columns(i)], gp_ref.at[:, columns(i)], g_send, g_recv.at[i],
            device_id=partner, device_id_type=MESH)

    def left(i):
        return pl.ds(pl.multiple_of(i * CHUNK, LANES), LANES)

    def right(i):
        return pl.ds(pl.multiple_of(i * CHUNK + LANES, LANES), LANES)

    def slab(k):
        return pl.ds(k * part, part)

    def y_copy(k, col, dst_ref, sem, to):
        return pltpu.make_async_remote_copy(
            p_ref.at[slab(k), col], dst_ref.at[:, col], y_send, sem, device_id=to, device_id_type=MESH)

    def product(i):
        p_ref[:, columns(i)] = (
            jnp.dot(ot_ref[...], g_ref[:, columns(i)], preferred_element_type=F32)
            + jnp.dot(pt_ref[...], gp_ref[:, columns(i)], preferred_element_type=F32)).astype(BF16)

    def first_sends(i):
        y_copy(2, left(i), f_ref, f_recv.at[i, 0], down).start()
        y_copy(2, right(i), f_ref, f_recv.at[i, 1], up).start()
        y_copy(1, left(i), o_ref, o_recv, up).start()
        y_copy(3, right(i), o_ref, o_recv, down).start()

    grads(0)
    g_copy(0).start()
    wait_bytes(pt_ref, pt_recv)

    @pl.loop(1, chunks)
    def _(i):
        grads(i)
        g_copy(i).start()
        g_copy(i - 1).wait_recv()
        product(i - 1)
        first_sends(i - 1)

    g_copy(chunks - 1).wait_recv()
    product(chunks - 1)
    first_sends(chunks - 1)

    @pl.loop(0, depth // CHUNK)
    def _(n):
        block = pl.ds(pl.multiple_of(n * CHUNK, CHUNK), CHUNK)
        gn_ref[:, block] = lax.dot_general(
            g_ref[...], u_ref[block, :], (((1,), (1,)), ((), ())), preferred_element_type=F32).astype(BF16)

    @pl.loop(1, n_t)
    def _(k):
        peer = lax.rem(t + k, n_t)
        pltpu.make_async_remote_copy(
            gn_ref.at[pl.ds(pl.multiple_of(peer * owned, owned), owned)], gr_ref.at[k], n_send, n_recv,
            device_id=(dp, peer), device_id_type=MESH).start()

    def add_hop(i, side):
        k, col = (3, left(i)) if side == 0 else (1, right(i))
        p_ref[slab(k), col] = (p_ref[slab(k), col].astype(F32) + f_ref[:, col].astype(F32)).astype(BF16)
        y_copy(k, col, out_s, s_recv, down if side == 0 else up).start()

    @pl.loop(0, chunks)
    def _(i):
        y_copy(2, left(i), f_ref, f_recv.at[i, 0], down).wait_recv()
        add_hop(i, 0)
        y_copy(2, right(i), f_ref, f_recv.at[i, 1], up).wait_recv()
        add_hop(i, 1)

    wait_bytes(o_ref, o_recv)

    @pl.loop(0, chunks)
    def _(i):
        cols = columns(i)
        p_ref[slab(0), cols] = (p_ref[slab(0), cols].astype(F32) + o_ref[:, cols].astype(F32)).astype(BF16)

    a_copy = pltpu.make_async_copy(p_ref.at[slab(0)], out_a, a_sem)
    a_copy.start()

    wait_bytes(gr_ref.at[pl.ds(0, n_t - 1)], n_recv)
    own = pl.ds(pl.multiple_of(t * owned, owned), owned)
    grad = gn_ref[own, :].astype(F32)
    for k in range(1, n_t):
        grad += gr_ref[k].astype(F32)
    hidden = hid_ref[...].astype(F32)
    inverse = lax.rsqrt(jnp.mean(hidden * hidden, axis=-1, keepdims=True) + 1e-06)
    normed = hidden * inverse
    grad = grad * gain_ref[...][None, :]
    inner = jnp.mean(grad * normed, axis=-1, keepdims=True)
    out_h[...] = (inverse * (grad - normed * inner)).astype(BF16)

    a_copy.wait()
    wait_bytes(out_s, s_recv)
    for part_sent in (sc_ref.at[0], sc_ref.at[0], sc_ref.at[3], sc_ref.at[0, 0, pl.ds(0, 3)], sc_ref.at[0, 0, pl.ds(0, 3)]):
        wait_bytes(part_sent, ag_send)
    wait_bytes(vst_ref.at[pl.ds(0, n_t - 1)], vs_send)
    wait_bytes(dst_ref.at[pl.ds(0, n_t - 1)], ds_send)
    wait_bytes(pt_ref, pt_send)
    wait_bytes(g_ref, g_send)
    wait_bytes(p_ref.at[pl.ds(0, 3 * part)], y_send)
    wait_bytes(gr_ref.at[pl.ds(0, n_t - 1)], n_send)


def finish(own_ref, sent_ref, hid_ref, out_u, out_h):
    out_u[...] = (own_ref[...].astype(F32) + sent_ref[...].astype(F32)).astype(BF16)
    out_h[...] = hid_ref[...]


def body(n_dp, n_t, hidden, norm_gain, unembed, verifier_logits, served_ids, accepted):
    owned, depth = hidden.shape
    rows, width = verifier_logits.shape
    part = depth // n_dp
    chunks = width // CHUNK
    vmem = pl.BlockSpec(memory_space=pltpu.VMEM)
    hbm = pl.BlockSpec(memory_space=pl.ANY)
    dma = pltpu.SemaphoreType.DMA
    own, sent, grad_hidden = pl.pallas_call(
        functools.partial(kernel, n_dp, n_t),
        out_shape=(
            jax.ShapeDtypeStruct((part, width), BF16),
            jax.ShapeDtypeStruct((part, width), BF16),
            jax.ShapeDtypeStruct((owned, depth), BF16),
        ),
        in_specs=[vmem, vmem, hbm, hbm, vmem, vmem],
        out_specs=(hbm, hbm, vmem),
        scratch_shapes=[
            pltpu.VMEM((rows, CHUNK), F32),
            pltpu.VMEM((rows, CHUNK), F32),
            pltpu.VMEM((depth, width), BF16),
            pltpu.VMEM((rows, width), BF16),
            pltpu.VMEM((rows, width), BF16),
            pltpu.VMEM((rows, width), BF16),
            pltpu.VMEM((SIDE, 2, SIDE, owned // 2, depth), BF16),
            pltpu.VMEM((depth, rows), BF16),
            pltpu.VMEM((depth // 2, rows), BF16),
            pltpu.VMEM((depth // 2, rows), BF16),
            pltpu.VMEM((depth // 2, width), BF16),
            pltpu.VMEM((part, width), BF16),
            pltpu.VMEM((part, width), BF16),
            pltpu.VMEM((rows, depth), BF16),
            pltpu.VMEM((n_t, owned, depth), BF16),
            pltpu.VMEM((rows, LANES), F32),
            pltpu.VMEM((rows, LANES), F32),
            pltpu.VMEM((rows, LANES), F32),
            pltpu.VMEM((rows, LANES), jnp.int32),
            pltpu.VMEM((rows, LANES), F32),
            pltpu.VMEM((rows, LANES), F32),
            pltpu.VMEM((rows, LANES), F32),
            pltpu.VMEM((rows, LANES), F32),
            pltpu.VMEM((n_t, 8, LANES), F32),
            pltpu.VMEM((n_t, 8, LANES), F32),
            dma, dma((chunks,)), dma, dma((WAVES, 2, SIDE)), dma((WAVES, 2, SIDE, 2)), dma((WAVES,)), dma, dma, dma, dma, dma, dma,
            dma, dma((chunks,)), dma, dma((chunks, 2)), dma, dma, dma, dma, dma,
        ],
        compiler_params=pltpu.CompilerParams(
            collective_id=0, has_side_effects=True, vmem_limit_bytes=62 * 1024 * 1024),
        cost_estimate=pl.CostEstimate(
            flops=6 * rows * depth * width, bytes_accessed=2 * (depth + rows + part) * width,
            transcendentals=4 * rows * width),
    )(hidden, norm_gain, unembed, verifier_logits, served_ids.reshape(rows // LANES, LANES), accepted.reshape(1, rows // DRAFT))
    steps = 4
    block = pl.BlockSpec((part // steps, width), lambda i: (i, 0))
    small = pl.BlockSpec((owned, depth), lambda i: (0, 0))
    return pl.pallas_call(
        finish,
        grid=(steps,),
        out_shape=(
            jax.ShapeDtypeStruct((part, width), BF16),
            jax.ShapeDtypeStruct((owned, depth), BF16),
        ),
        in_specs=[block, block, small],
        out_specs=(block, small),
        compiler_params=pltpu.CompilerParams(vmem_limit_bytes=62 * 1024 * 1024),
    )(own, sent, grad_hidden)


def solution(mesh):
    n_dp, n_t = mesh.shape["dp"], mesh.shape["tensor"]

    def run(*args):
        return body(n_dp, n_t, *args)

    return jax.shard_map(
        run,
        mesh=mesh,
        in_specs=(
            P(("dp", "tensor"), None),
            P(),
            P(None, "tensor"),
            P("dp", "tensor"),
            P("dp"),
            P("dp"),
        ),
        out_specs=(P("dp", "tensor"), P(("dp", "tensor"), None)),
        check_vma=False,
    )
```

```python
import functools

import jax
import jax.numpy as jnp
from jax import lax
from jax.experimental import pallas as pl
from jax.experimental.pallas import tpu as pltpu
from jax.sharding import PartitionSpec as P

DRAFT = 8
SIDE = 4
WAVES = 1
DIRECT = (2, 3)
FAR_FIRST = sorted(
    ((dz, dx) for dz in range(SIDE) for dx in range(SIDE) if dz or dx),
    key=lambda d: -sum(min(c, SIDE - c) for c in d))
LOG_LOW = -1.6094379124341003
MESH = pl.DeviceIdType.MESH
F32 = jnp.float32
BF16 = jnp.bfloat16
LANES = 128
CHUNK = 256


def wait_bytes(ref, sem):
    pltpu.make_async_copy(ref, ref, sem).wait()


def to_columns(row):
    return jnp.transpose(jnp.broadcast_to(row, (LANES, LANES)))


def log_sum_rows(ref, index, lse_ref):
    block, width = 32, ref.shape[1]
    at = pl.ds(pl.multiple_of(index * block, block), block)
    tops = [ref[at, j * LANES:(j + 1) * LANES].astype(F32) for j in range(2)]
    for j in range(2, width // LANES):
        tops[j % 2] = jnp.maximum(tops[j % 2], ref[at, j * LANES:(j + 1) * LANES].astype(F32))
    top = jnp.max(jnp.maximum(tops[0], tops[1]), axis=-1, keepdims=True)
    wide = jnp.broadcast_to(top, (block, LANES))
    sums = [jnp.zeros((block, LANES), F32) for _ in range(2)]
    for j in range(width // LANES):
        sums[j % 2] += jnp.exp(ref[at, j * LANES:(j + 1) * LANES].astype(F32) - wide)
    total = jnp.sum(sums[0] + sums[1], axis=-1, keepdims=True)
    lse_ref[at, :] = jnp.broadcast_to(top + jnp.log(total), (block, LANES))


def pack_rows(lse_ref, stat_ref, rows):
    same = lax.broadcasted_iota(jnp.int32, (LANES, LANES), 0) == lax.broadcasted_iota(jnp.int32, (LANES, LANES), 1)
    for b in range(rows // LANES):
        picked = jnp.where(same, lse_ref[b * LANES:(b + 1) * LANES, :], 0.0)
        stat_ref[0, b:b + 1, :] = jnp.sum(picked, axis=0, keepdims=True)


def combine(stat_ref):
    stats = stat_ref[...]
    top = jnp.max(stats, axis=0)
    return top + jnp.log(jnp.sum(jnp.exp(stats - top[None]), axis=0))


def kernel(n_dp, n_t, hid_ref, gain_ref, u_hbm, v_hbm, ids_ref, acc_ref, out_a, out_s, out_h,
           even_ref, odd_ref, u_ref, v_ref, g_ref, gp_ref, sc_ref, tr_ref, ot_ref, pt_ref, p_ref, f_ref, o_ref,
           gn_ref, gr_ref, lse_ref, a_ref, b_ref, i_ref, w_ref, lw_ref, m_ref, z_ref, vst_ref, dst_ref,
           v_sem, u_sem, ag_send, r1_sem, r2_sem, r3_sem, vs_send, vs_recv, ds_send, ds_recv, pt_send, pt_recv,
           g_send, g_recv, y_send, f_recv, o_recv, s_recv, a_sem, n_send, n_recv):
    rows, width = v_ref.shape
    owned, depth = hid_ref.shape
    chunks = width // CHUNK
    part = out_a.shape[0]
    n_y = n_dp // 2
    dp, t = lax.axis_index("dp"), lax.axis_index("tensor")
    y, core = dp // 2, lax.rem(dp, 2)
    partner = (dp + 1 - 2 * core, t)
    up = (lax.rem(dp + 2, n_dp), t)
    down = (lax.rem(dp + n_dp - 2, n_dp), t)

    z, x = t // SIDE, lax.rem(t, SIDE)

    def peer(dz, dx):
        return (dp, lax.rem(z + dz, SIDE) * SIDE + lax.rem(x + dx, SIDE))

    barrier = pltpu.get_barrier_semaphore()
    for dz, dx in FAR_FIRST:
        pl.semaphore_signal(barrier, inc=1, device_id=peer(dz, dx), device_id_type=MESH)
    for other in (partner, up, down):
        pl.semaphore_signal(barrier, inc=1, device_id=other, device_id_type=MESH)

    v_copy = pltpu.make_async_copy(v_hbm, v_ref, v_sem)
    v_copy.start()

    def columns(i):
        return pl.ds(pl.multiple_of(i * CHUNK, CHUNK), CHUNK)

    def u_copy(i):
        return pltpu.make_async_copy(u_hbm.at[:, columns(i)], u_ref.at[:, columns(i)], u_sem.at[i])

    @pl.loop(0, chunks)
    def _(i):
        u_copy(i).start()

    place = (x, z)

    def first_axis(half, off):
        if half == 0:
            return (dp, z * SIDE + lax.rem(x + off, SIDE))
        return (dp, lax.rem(z + off, SIDE) * SIDE + x)

    def second_axis(half, off):
        return first_axis(1 - half, off)

    span = depth // WAVES

    def line_copy(w, half, off):
        block = sc_ref.at[0, half, place[half], :, pl.ds(w * span, span)]
        return pltpu.make_async_remote_copy(
            block, block, ag_send, r1_sem.at[w, half, off],
            device_id=first_axis(half, off), device_id_type=MESH)

    def cross_copy(w, half, off, back):
        o = lax.rem(place[half] + SIDE - off, SIDE)
        cols = pl.ds(w * span, span)
        return pltpu.make_async_remote_copy(
            sc_ref.at[0, half, o, :, cols], sc_ref.at[1 if back else 2, half, o, :, cols],
            ag_send, r2_sem.at[w, half, off, back],
            device_id=second_axis(half, SIDE - 1 if back else 1), device_id_type=MESH)

    def relay_copy(w, half, off, back):
        o = lax.rem(place[half] + SIDE - off, SIDE)
        cols = pl.ds(w * span + back * span // 2, span // 2)
        return pltpu.make_async_remote_copy(
            sc_ref.at[1 if back else 2, half, o, :, cols], sc_ref.at[3, half, o, :, cols], ag_send, r3_sem.at[w],
            device_id=second_axis(half, SIDE - 1 if back else 1), device_id_type=MESH)

    def far_copy(w, half, off):
        o = lax.rem(place[half] + SIDE - off, SIDE)
        return pltpu.make_async_remote_copy(
            sc_ref.at[0, half, o], sc_ref.at[3, half, o], ag_send, r3_sem.at[w],
            device_id=second_axis(half, 2), device_id_type=MESH)

    def begin(w):
        for off in (1, 3, 2):
            for half in range(2):
                line_copy(w, half, off).start()
        for half in range(2):
            for back in range(2):
                cross_copy(w, half, 0, back).start()

    def forward_cross(w, off):
        for half in range(2):
            line_copy(w, half, off).wait_recv()
            if off in DIRECT:
                far_copy(w, half, off).start()
            for back in range(2):
                cross_copy(w, half, off, back).start()

    def forward_relay(w, off):
        for half in range(2):
            for back in range(2):
                cross_copy(w, half, off, back).wait_recv()
                if off not in DIRECT:
                    relay_copy(w, half, off, back).start()

    def gathered(w):
        wait_bytes(sc_ref.at[3, :, :, :, pl.ds(w * span, span)], r3_sem.at[w])

    def verifier(first, last):
        @pl.loop(first, last)
        def _(i):
            log_sum_rows(v_ref, i, lse_ref)

    hidden = hid_ref[...].astype(F32)
    inverse = lax.rsqrt(jnp.mean(hidden * hidden, axis=-1, keepdims=True) + 1e-06)
    scaled = (hidden * inverse * gain_ref[...][None, :]).astype(BF16)
    for half in range(2):
        sc_ref[0, half, place[half]] = scaled[half * owned // 2:(half + 1) * owned // 2]
    pl.semaphore_wait(barrier, n_t + 2)

    begin(0)
    m_ref[...] = jnp.full(m_ref.shape, -jnp.inf, F32)
    z_ref[...] = jnp.zeros(z_ref.shape, F32)
    vst_ref[0] = jnp.zeros(vst_ref.shape[1:], F32)
    dst_ref[0] = jnp.zeros(dst_ref.shape[1:], F32)
    blocks = rows // DRAFT
    for b in range(rows // LANES):
        at = slice(b * LANES, (b + 1) * LANES)
        row = b * LANES + lax.broadcasted_iota(jnp.int32, (LANES, blocks), 0)
        same = lax.shift_right_logical(row, 3) == lax.broadcasted_iota(jnp.int32, (LANES, blocks), 1)
        count = jnp.sum(jnp.where(same, acc_ref[...].astype(F32), 0.0), axis=-1, keepdims=True)
        slot = (lax.broadcasted_iota(jnp.int32, (LANES, LANES), 0) & (DRAFT - 1)).astype(F32)
        kept = slot <= jnp.broadcast_to(count, (LANES, LANES))
        lw_ref[at, :] = jnp.where(kept, 0.0, LOG_LOW)
        w_ref[at, :] = jnp.where(kept, 0.2, 0.2 * 0.2)
        i_ref[at, :] = to_columns(ids_ref[b:b + 1, :] - t * width)

    v_copy.wait()
    forward_cross(0, 1)
    forward_cross(0, 3)
    verifier(0, 3)
    forward_relay(0, 0)
    verifier(3, 6)
    forward_cross(0, 2)
    verifier(6, 9)
    forward_relay(0, 1)
    verifier(9, 11)
    forward_relay(0, 3)
    verifier(11, 13)
    forward_relay(0, 2)
    verifier(13, rows // 32)
    pack_rows(lse_ref, vst_ref, rows)

    for dz, dx in FAR_FIRST:
        pltpu.make_async_remote_copy(
            vst_ref.at[0], vst_ref.at[dz * SIDE + dx], vs_send, vs_recv,
            device_id=peer(dz, dx), device_id_type=MESH).start()

    gathered(0)

    @pl.loop(0, chunks)
    def _(i):
        u_copy(i).wait()

    quarter = rows // SIDE

    def home(block):
        slot, half, o = block // 8, block // 4 % 2, block % 4
        far = lax.rem(place[1 - half] + (0, 1, SIDE - 1, 2)[slot], SIDE)
        if half == 0:
            return pl.multiple_of(far * quarter + o * owned, 16)
        return pl.multiple_of(o * quarter + far * owned + 16, 16)

    def drafter(i, buf):
        buf[...] = jnp.dot(sc_ref[...].reshape(rows, depth), u_ref[:, columns(i)], preferred_element_type=F32)

    def gather_stats(i, buf):
        for b in range(rows // 32):
            at = slice(b * 32, (b + 1) * 32)
            logits = buf[at, :].astype(BF16)
            for h in range(2):
                g_ref[pl.ds(home(2 * b + h), 16), columns(i)] = logits[h * 16:(h + 1) * 16]
            piece = logits.astype(F32)
            tiles = [piece[:, j * LANES:(j + 1) * LANES] for j in range(CHUNK // LANES)]
            old = m_ref[at, :]
            top = old
            for tile in tiles:
                top = jnp.maximum(top, tile)
            total = z_ref[at, :] * jnp.exp(old - top)
            for tile in tiles:
                total += jnp.exp(tile - top)
            m_ref[at, :] = top
            z_ref[at, :] = total

    drafter(0, even_ref)

    @pl.loop(0, chunks // 2)
    def _(j):
        drafter(2 * j + 1, odd_ref)
        gather_stats(2 * j, even_ref)
        drafter(2 * j + 2, even_ref)
        gather_stats(2 * j + 1, odd_ref)

    gather_stats(chunks - 1, even_ref)

    for b in range(rows // 16):
        at = slice(b * 16, (b + 1) * 16)
        top = jnp.max(m_ref[at, :], axis=-1, keepdims=True)
        total = jnp.sum(z_ref[at, :] * jnp.exp(m_ref[at, :] - top), axis=-1, keepdims=True)
        lse_ref[pl.ds(home(b), 16), :] = jnp.broadcast_to(top + jnp.log(total), (16, LANES))
    pack_rows(lse_ref, dst_ref, rows)

    for dz, dx in FAR_FIRST:
        pltpu.make_async_remote_copy(
            dst_ref.at[0], dst_ref.at[dz * SIDE + dx], ds_send, ds_recv,
            device_id=peer(dz, dx), device_id_type=MESH).start()

    for b in range(rows // 16):
        gn_ref[pl.ds(home(b), 16), :] = sc_ref[b // 8, b // 4 % 2, b % 4]

    @pl.loop(0, depth // CHUNK)
    def _(i):
        tr_ref[columns(i), :] = jnp.transpose(gn_ref[:, columns(i)])

    def pt_copy(k):
        block = pl.ds(pl.multiple_of((2 * lax.rem(y + k, n_y) + 1 - core) * part, 16), part)
        return pltpu.make_async_remote_copy(
            tr_ref.at[block], pt_ref.at[pl.ds(k * part, part)], pt_send, pt_recv,
            device_id=partner, device_id_type=MESH)

    for k in range(n_y):
        pt_copy(k).start()
    for k in range(n_y):
        block = pl.ds(pl.multiple_of((2 * lax.rem(y + k, n_y) + core) * part, 16), part)
        ot_ref[k * part:(k + 1) * part, :] = tr_ref[block, :]

    wait_bytes(vst_ref.at[pl.ds(0, n_t - 1)], vs_recv)
    verif_off = combine(vst_ref) - jnp.log(F32(0.8))
    for b in range(rows // LANES):
        at = slice(b * LANES, (b + 1) * LANES)
        b_ref[at, :] = to_columns(verif_off[b:b + 1]) - lw_ref[at, :]
    wait_bytes(dst_ref.at[pl.ds(0, n_t - 1)], ds_recv)
    draft_off = combine(dst_ref)
    for b in range(rows // LANES):
        at = slice(b * LANES, (b + 1) * LANES)
        a_ref[at, :] = to_columns(draft_off[b:b + 1]) - lw_ref[at, :]

    lane = lax.broadcasted_iota(jnp.int32, (64, LANES), 1)

    def grads(i):
        for b in range(rows // 64):
            at = slice(b * 64, (b + 1) * 64)
            for j in range(CHUNK // LANES):
                col = pl.ds(pl.multiple_of(i * CHUNK + j * LANES, LANES), LANES)
                draft = jnp.exp(g_ref[at, col].astype(F32) - a_ref[at, :])
                verif = jnp.exp(v_ref[at, col].astype(F32) - b_ref[at, :])
                hit = i_ref[at, :] - (i * CHUNK + j * LANES) == lane
                g_ref[at, col] = (draft - verif - jnp.where(hit, w_ref[at, :], 0.0)).astype(BF16)

    def g_copy(i):
        return pltpu.make_async_remote_copy(
            g_ref.at[:, columns(i)], gp_ref.at[:, columns(i)], g_send, g_recv.at[i],
            device_id=partner, device_id_type=MESH)

    def left(i):
        return pl.ds(pl.multiple_of(i * CHUNK, LANES), LANES)

    def right(i):
        return pl.ds(pl.multiple_of(i * CHUNK + LANES, LANES), LANES)

    def slab(k):
        return pl.ds(k * part, part)

    def y_copy(k, col, dst_ref, sem, to):
        return pltpu.make_async_remote_copy(
            p_ref.at[slab(k), col], dst_ref.at[:, col], y_send, sem, device_id=to, device_id_type=MESH)

    def product(i):
        p_ref[:, columns(i)] = (
            jnp.dot(ot_ref[...], g_ref[:, columns(i)], preferred_element_type=F32)
            + jnp.dot(pt_ref[...], gp_ref[:, columns(i)], preferred_element_type=F32)).astype(BF16)

    def first_sends(i):
        y_copy(2, left(i), f_ref, f_recv.at[i, 0], down).start()
        y_copy(2, right(i), f_ref, f_recv.at[i, 1], up).start()
        y_copy(1, left(i), o_ref, o_recv, up).start()
        y_copy(3, right(i), o_ref, o_recv, down).start()

    grads(0)
    g_copy(0).start()
    wait_bytes(pt_ref, pt_recv)

    @pl.loop(1, chunks)
    def _(i):
        grads(i)
        g_copy(i).start()
        g_copy(i - 1).wait_recv()
        product(i - 1)
        first_sends(i - 1)

    g_copy(chunks - 1).wait_recv()
    product(chunks - 1)
    first_sends(chunks - 1)

    @pl.loop(0, depth // CHUNK)
    def _(n):
        block = pl.ds(pl.multiple_of(n * CHUNK, CHUNK), CHUNK)
        gn_ref[:, block] = lax.dot_general(
            g_ref[...], u_ref[block, :], (((1,), (1,)), ((), ())), preferred_element_type=F32).astype(BF16)

    @pl.loop(1, n_t)
    def _(k):
        peer = lax.rem(t + k, n_t)
        pltpu.make_async_remote_copy(
            gn_ref.at[pl.ds(pl.multiple_of(peer * owned, owned), owned)], gr_ref.at[k], n_send, n_recv,
            device_id=(dp, peer), device_id_type=MESH).start()

    def add_hop(i, side):
        k, col = (3, left(i)) if side == 0 else (1, right(i))
        p_ref[slab(k), col] = (p_ref[slab(k), col].astype(F32) + f_ref[:, col].astype(F32)).astype(BF16)
        y_copy(k, col, out_s, s_recv, down if side == 0 else up).start()

    @pl.loop(0, chunks)
    def _(i):
        y_copy(2, left(i), f_ref, f_recv.at[i, 0], down).wait_recv()
        add_hop(i, 0)
        y_copy(2, right(i), f_ref, f_recv.at[i, 1], up).wait_recv()
        add_hop(i, 1)

    wait_bytes(o_ref, o_recv)

    @pl.loop(0, chunks)
    def _(i):
        cols = columns(i)
        p_ref[slab(0), cols] = (p_ref[slab(0), cols].astype(F32) + o_ref[:, cols].astype(F32)).astype(BF16)

    a_copy = pltpu.make_async_copy(p_ref.at[slab(0)], out_a, a_sem)
    a_copy.start()

    wait_bytes(gr_ref.at[pl.ds(0, n_t - 1)], n_recv)
    own = pl.ds(pl.multiple_of(t * owned, owned), owned)
    grad = gn_ref[own, :].astype(F32)
    for k in range(1, n_t):
        grad += gr_ref[k].astype(F32)
    hidden = hid_ref[...].astype(F32)
    inverse = lax.rsqrt(jnp.mean(hidden * hidden, axis=-1, keepdims=True) + 1e-06)
    normed = hidden * inverse
    grad = grad * gain_ref[...][None, :]
    inner = jnp.mean(grad * normed, axis=-1, keepdims=True)
    out_h[...] = (inverse * (grad - normed * inner)).astype(BF16)

    a_copy.wait()
    wait_bytes(out_s, s_recv)
    for part_sent in (sc_ref.at[0], sc_ref.at[0], sc_ref.at[3], sc_ref.at[0, 0, pl.ds(0, 3)], sc_ref.at[0, 0, pl.ds(0, 3)]):
        wait_bytes(part_sent, ag_send)
    wait_bytes(vst_ref.at[pl.ds(0, n_t - 1)], vs_send)
    wait_bytes(dst_ref.at[pl.ds(0, n_t - 1)], ds_send)
    wait_bytes(pt_ref, pt_send)
    wait_bytes(g_ref, g_send)
    wait_bytes(p_ref.at[pl.ds(0, 3 * part)], y_send)
    wait_bytes(gr_ref.at[pl.ds(0, n_t - 1)], n_send)


def finish(own_ref, sent_ref, hid_ref, out_u, out_h):
    out_u[...] = (own_ref[...].astype(F32) + sent_ref[...].astype(F32)).astype(BF16)
    out_h[...] = hid_ref[...]


def body(n_dp, n_t, hidden, norm_gain, unembed, verifier_logits, served_ids, accepted):
    owned, depth = hidden.shape
    rows, width = verifier_logits.shape
    part = depth // n_dp
    chunks = width // CHUNK
    vmem = pl.BlockSpec(memory_space=pltpu.VMEM)
    hbm = pl.BlockSpec(memory_space=pl.ANY)
    dma = pltpu.SemaphoreType.DMA
    own, sent, grad_hidden = pl.pallas_call(
        functools.partial(kernel, n_dp, n_t),
        out_shape=(
            jax.ShapeDtypeStruct((part, width), BF16),
            jax.ShapeDtypeStruct((part, width), BF16),
            jax.ShapeDtypeStruct((owned, depth), BF16),
        ),
        in_specs=[vmem, vmem, hbm, hbm, vmem, vmem],
        out_specs=(hbm, hbm, vmem),
        scratch_shapes=[
            pltpu.VMEM((rows, CHUNK), F32),
            pltpu.VMEM((rows, CHUNK), F32),
            pltpu.VMEM((depth, width), BF16),
            pltpu.VMEM((rows, width), BF16),
            pltpu.VMEM((rows, width), BF16),
            pltpu.VMEM((rows, width), BF16),
            pltpu.VMEM((SIDE, 2, SIDE, owned // 2, depth), BF16),
            pltpu.VMEM((depth, rows), BF16),
            pltpu.VMEM((depth // 2, rows), BF16),
            pltpu.VMEM((depth // 2, rows), BF16),
            pltpu.VMEM((depth // 2, width), BF16),
            pltpu.VMEM((part, width), BF16),
            pltpu.VMEM((part, width), BF16),
            pltpu.VMEM((rows, depth), BF16),
            pltpu.VMEM((n_t, owned, depth), BF16),
            pltpu.VMEM((rows, LANES), F32),
            pltpu.VMEM((rows, LANES), F32),
            pltpu.VMEM((rows, LANES), F32),
            pltpu.VMEM((rows, LANES), jnp.int32),
            pltpu.VMEM((rows, LANES), F32),
            pltpu.VMEM((rows, LANES), F32),
            pltpu.VMEM((rows, LANES), F32),
            pltpu.VMEM((rows, LANES), F32),
            pltpu.VMEM((n_t, 8, LANES), F32),
            pltpu.VMEM((n_t, 8, LANES), F32),
            dma, dma((chunks,)), dma, dma((WAVES, 2, SIDE)), dma((WAVES, 2, SIDE, 2)), dma((WAVES,)), dma, dma, dma, dma, dma, dma,
            dma, dma((chunks,)), dma, dma((chunks, 2)), dma, dma, dma, dma, dma,
        ],
        compiler_params=pltpu.CompilerParams(
            collective_id=0, has_side_effects=True, vmem_limit_bytes=62 * 1024 * 1024),
        cost_estimate=pl.CostEstimate(
            flops=6 * rows * depth * width, bytes_accessed=2 * (depth + rows + part) * width,
            transcendentals=4 * rows * width),
    )(hidden, norm_gain, unembed, verifier_logits, served_ids.reshape(rows // LANES, LANES), accepted.reshape(1, rows // DRAFT))
    steps = 4
    block = pl.BlockSpec((part // steps, width), lambda i: (i, 0))
    small = pl.BlockSpec((owned, depth), lambda i: (0, 0))
    return pl.pallas_call(
        finish,
        grid=(steps,),
        out_shape=(
            jax.ShapeDtypeStruct((part, width), BF16),
            jax.ShapeDtypeStruct((owned, depth), BF16),
        ),
        in_specs=[block, block, small],
        out_specs=(block, small),
        compiler_params=pltpu.CompilerParams(vmem_limit_bytes=62 * 1024 * 1024),
    )(own, sent, grad_hidden)


def solution(mesh):
    n_dp, n_t = mesh.shape["dp"], mesh.shape["tensor"]

    def run(*args):
        return body(n_dp, n_t, *args)

    return jax.shard_map(
        run,
        mesh=mesh,
        in_specs=(
            P(("dp", "tensor"), None),
            P(),
            P(None, "tensor"),
            P("dp", "tensor"),
            P("dp"),
            P("dp"),
        ),
        out_specs=(P("dp", "tensor"), P(("dp", "tensor"), None)),
        check_vma=False,
    )
```

```python
import functools

import jax
import jax.numpy as jnp
from jax import lax
from jax.experimental import pallas as pl
from jax.experimental.pallas import tpu as pltpu
from jax.sharding import PartitionSpec as P

DRAFT = 8
SIDE = 4
WAVES = 1
DIRECT = (2, 3)
FAR_FIRST = sorted(
    ((dz, dx) for dz in range(SIDE) for dx in range(SIDE) if dz or dx),
    key=lambda d: -sum(min(c, SIDE - c) for c in d))
LOG_LOW = -1.6094379124341003
MESH = pl.DeviceIdType.MESH
F32 = jnp.float32
BF16 = jnp.bfloat16
LANES = 128
CHUNK = 256


def wait_bytes(ref, sem):
    pltpu.make_async_copy(ref, ref, sem).wait()


def to_columns(row):
    return jnp.transpose(jnp.broadcast_to(row, (LANES, LANES)))


def log_sum_rows(ref, index, lse_ref):
    block, width = 32, ref.shape[1]
    at = pl.ds(pl.multiple_of(index * block, block), block)
    tops = [ref[at, j * LANES:(j + 1) * LANES].astype(F32) for j in range(2)]
    for j in range(2, width // LANES):
        tops[j % 2] = jnp.maximum(tops[j % 2], ref[at, j * LANES:(j + 1) * LANES].astype(F32))
    top = jnp.max(jnp.maximum(tops[0], tops[1]), axis=-1, keepdims=True)
    wide = jnp.broadcast_to(top, (block, LANES))
    sums = [jnp.zeros((block, LANES), F32) for _ in range(2)]
    for j in range(width // LANES):
        sums[j % 2] += jnp.exp(ref[at, j * LANES:(j + 1) * LANES].astype(F32) - wide)
    total = jnp.sum(sums[0] + sums[1], axis=-1, keepdims=True)
    lse_ref[at, :] = jnp.broadcast_to(top + jnp.log(total), (block, LANES))


def pack_rows(lse_ref, stat_ref, rows):
    same = lax.broadcasted_iota(jnp.int32, (LANES, LANES), 0) == lax.broadcasted_iota(jnp.int32, (LANES, LANES), 1)
    for b in range(rows // LANES):
        picked = jnp.where(same, lse_ref[b * LANES:(b + 1) * LANES, :], 0.0)
        stat_ref[0, b:b + 1, :] = jnp.sum(picked, axis=0, keepdims=True)


def combine(stat_ref):
    stats = stat_ref[...]
    top = jnp.max(stats, axis=0)
    return top + jnp.log(jnp.sum(jnp.exp(stats - top[None]), axis=0))


def kernel(n_dp, n_t, hid_ref, gain_ref, u_hbm, v_hbm, ids_ref, acc_ref, out_a, out_s, out_h,
           even_ref, odd_ref, u_ref, v_ref, g_ref, gp_ref, sc_ref, tr_ref, ot_ref, pt_ref, p_ref, f_ref, o_ref,
           gn_ref, gr_ref, lse_ref, a_ref, b_ref, i_ref, w_ref, lw_ref, m_ref, z_ref, vst_ref, dst_ref,
           v_sem, u_sem, ag_send, r1_sem, r2_sem, r3_sem, vs_send, vs_recv, ds_send, ds_recv, pt_send, pt_recv,
           g_send, g_recv, y_send, f_recv, o_recv, s_recv, a_sem, n_send, n_recv):
    rows, width = v_ref.shape
    owned, depth = hid_ref.shape
    chunks = width // CHUNK
    part = out_a.shape[0]
    n_y = n_dp // 2
    dp, t = lax.axis_index("dp"), lax.axis_index("tensor")
    y, core = dp // 2, lax.rem(dp, 2)
    partner = (dp + 1 - 2 * core, t)
    up = (lax.rem(dp + 2, n_dp), t)
    down = (lax.rem(dp + n_dp - 2, n_dp), t)

    z, x = t // SIDE, lax.rem(t, SIDE)

    def peer(dz, dx):
        return (dp, lax.rem(z + dz, SIDE) * SIDE + lax.rem(x + dx, SIDE))

    barrier = pltpu.get_barrier_semaphore()
    for dz, dx in FAR_FIRST:
        pl.semaphore_signal(barrier, inc=1, device_id=peer(dz, dx), device_id_type=MESH)
    for other in (partner, up, down):
        pl.semaphore_signal(barrier, inc=1, device_id=other, device_id_type=MESH)

    v_copy = pltpu.make_async_copy(v_hbm, v_ref, v_sem)
    v_copy.start()

    def columns(i):
        return pl.ds(pl.multiple_of(i * CHUNK, CHUNK), CHUNK)

    def u_copy(i):
        return pltpu.make_async_copy(u_hbm.at[:, columns(i)], u_ref.at[:, columns(i)], u_sem.at[i])

    @pl.loop(0, chunks)
    def _(i):
        u_copy(i).start()

    place = (x, z)

    def first_axis(half, off):
        if half == 0:
            return (dp, z * SIDE + lax.rem(x + off, SIDE))
        return (dp, lax.rem(z + off, SIDE) * SIDE + x)

    def second_axis(half, off):
        return first_axis(1 - half, off)

    span = depth // WAVES

    def line_copy(w, half, off):
        block = sc_ref.at[0, half, place[half], :, pl.ds(w * span, span)]
        return pltpu.make_async_remote_copy(
            block, block, ag_send, r1_sem.at[w, half, off],
            device_id=first_axis(half, off), device_id_type=MESH)

    def cross_copy(w, half, off, back):
        o = lax.rem(place[half] + SIDE - off, SIDE)
        cols = pl.ds(w * span, span)
        return pltpu.make_async_remote_copy(
            sc_ref.at[0, half, o, :, cols], sc_ref.at[1 if back else 2, half, o, :, cols],
            ag_send, r2_sem.at[w, half, off, back],
            device_id=second_axis(half, SIDE - 1 if back else 1), device_id_type=MESH)

    def relay_copy(w, half, off, back):
        o = lax.rem(place[half] + SIDE - off, SIDE)
        cols = pl.ds(w * span + back * span // 2, span // 2)
        return pltpu.make_async_remote_copy(
            sc_ref.at[1 if back else 2, half, o, :, cols], sc_ref.at[3, half, o, :, cols], ag_send, r3_sem.at[w],
            device_id=second_axis(half, SIDE - 1 if back else 1), device_id_type=MESH)

    def far_copy(w, half, off):
        o = lax.rem(place[half] + SIDE - off, SIDE)
        return pltpu.make_async_remote_copy(
            sc_ref.at[0, half, o], sc_ref.at[3, half, o], ag_send, r3_sem.at[w],
            device_id=second_axis(half, 2), device_id_type=MESH)

    def begin(w):
        for off in (1, 3, 2):
            for half in range(2):
                line_copy(w, half, off).start()
        for half in range(2):
            for back in range(2):
                cross_copy(w, half, 0, back).start()

    def forward_cross(w, off):
        for half in range(2):
            line_copy(w, half, off).wait_recv()
            if off in DIRECT:
                far_copy(w, half, off).start()
            for back in range(2):
                cross_copy(w, half, off, back).start()

    def forward_relay(w, off):
        for half in range(2):
            for back in range(2):
                cross_copy(w, half, off, back).wait_recv()
                if off not in DIRECT:
                    relay_copy(w, half, off, back).start()

    def gathered(w):
        wait_bytes(sc_ref.at[3, :, :, :, pl.ds(w * span, span)], r3_sem.at[w])

    def verifier(first, last):
        @pl.loop(first, last)
        def _(i):
            log_sum_rows(v_ref, i, lse_ref)

    hidden = hid_ref[...].astype(F32)
    inverse = lax.rsqrt(jnp.mean(hidden * hidden, axis=-1, keepdims=True) + 1e-06)
    scaled = (hidden * inverse * gain_ref[...][None, :]).astype(BF16)
    for half in range(2):
        sc_ref[0, half, place[half]] = scaled[half * owned // 2:(half + 1) * owned // 2]
    pl.semaphore_wait(barrier, n_t + 2)

    begin(0)
    m_ref[...] = jnp.full(m_ref.shape, -jnp.inf, F32)
    z_ref[...] = jnp.zeros(z_ref.shape, F32)
    vst_ref[0] = jnp.zeros(vst_ref.shape[1:], F32)
    dst_ref[0] = jnp.zeros(dst_ref.shape[1:], F32)
    blocks = rows // DRAFT
    for b in range(rows // LANES):
        at = slice(b * LANES, (b + 1) * LANES)
        row = b * LANES + lax.broadcasted_iota(jnp.int32, (LANES, blocks), 0)
        same = lax.shift_right_logical(row, 3) == lax.broadcasted_iota(jnp.int32, (LANES, blocks), 1)
        count = jnp.sum(jnp.where(same, acc_ref[...].astype(F32), 0.0), axis=-1, keepdims=True)
        slot = (lax.broadcasted_iota(jnp.int32, (LANES, LANES), 0) & (DRAFT - 1)).astype(F32)
        kept = slot <= jnp.broadcast_to(count, (LANES, LANES))
        lw_ref[at, :] = jnp.where(kept, 0.0, LOG_LOW)
        w_ref[at, :] = jnp.where(kept, 0.2, 0.2 * 0.2)
        i_ref[at, :] = to_columns(ids_ref[b:b + 1, :] - t * width)

    v_copy.wait()
    forward_cross(0, 1)
    forward_cross(0, 3)
    verifier(0, 3)
    forward_relay(0, 0)
    verifier(3, 6)
    forward_cross(0, 2)
    verifier(6, 9)
    forward_relay(0, 1)
    verifier(9, 11)
    forward_relay(0, 3)
    verifier(11, 13)
    forward_relay(0, 2)
    verifier(13, rows // 32)
    pack_rows(lse_ref, vst_ref, rows)

    for dz, dx in FAR_FIRST:
        pltpu.make_async_remote_copy(
            vst_ref.at[0], vst_ref.at[dz * SIDE + dx], vs_send, vs_recv,
            device_id=peer(dz, dx), device_id_type=MESH).start()

    gathered(0)

    @pl.loop(0, chunks)
    def _(i):
        u_copy(i).wait()

    quarter = rows // SIDE

    def home(block):
        slot, half, o = block // 8, block // 4 % 2, block % 4
        far = lax.rem(place[1 - half] + (0, 1, SIDE - 1, 2)[slot], SIDE)
        if half == 0:
            return pl.multiple_of(far * quarter + o * owned, 16)
        return pl.multiple_of(o * quarter + far * owned + 16, 16)

    def drafter(i, buf):
        buf[...] = jnp.dot(sc_ref[...].reshape(rows, depth), u_ref[:, columns(i)], preferred_element_type=F32)

    def gather_stats(i, buf):
        for b in range(rows // 32):
            at = slice(b * 32, (b + 1) * 32)
            logits = buf[at, :].astype(BF16)
            for h in range(2):
                g_ref[pl.ds(home(2 * b + h), 16), columns(i)] = logits[h * 16:(h + 1) * 16]
            piece = logits.astype(F32)
            tiles = [piece[:, j * LANES:(j + 1) * LANES] for j in range(CHUNK // LANES)]
            old = m_ref[at, :]
            top = old
            for tile in tiles:
                top = jnp.maximum(top, tile)
            total = z_ref[at, :] * jnp.exp(old - top)
            for tile in tiles:
                total += jnp.exp(tile - top)
            m_ref[at, :] = top
            z_ref[at, :] = total

    drafter(0, even_ref)

    @pl.loop(0, chunks // 2)
    def _(j):
        drafter(2 * j + 1, odd_ref)
        gather_stats(2 * j, even_ref)
        drafter(2 * j + 2, even_ref)
        gather_stats(2 * j + 1, odd_ref)

    gather_stats(chunks - 1, even_ref)

    for b in range(rows // 16):
        at = slice(b * 16, (b + 1) * 16)
        top = jnp.max(m_ref[at, :], axis=-1, keepdims=True)
        total = jnp.sum(z_ref[at, :] * jnp.exp(m_ref[at, :] - top), axis=-1, keepdims=True)
        lse_ref[pl.ds(home(b), 16), :] = jnp.broadcast_to(top + jnp.log(total), (16, LANES))
    pack_rows(lse_ref, dst_ref, rows)

    for dz, dx in FAR_FIRST:
        pltpu.make_async_remote_copy(
            dst_ref.at[0], dst_ref.at[dz * SIDE + dx], ds_send, ds_recv,
            device_id=peer(dz, dx), device_id_type=MESH).start()

    for b in range(rows // 16):
        gn_ref[pl.ds(home(b), 16), :] = sc_ref[b // 8, b // 4 % 2, b % 4]

    @pl.loop(0, depth // CHUNK)
    def _(i):
        tr_ref[columns(i), :] = jnp.transpose(gn_ref[:, columns(i)])

    def pt_copy(k):
        block = pl.ds(pl.multiple_of((2 * lax.rem(y + k, n_y) + 1 - core) * part, 16), part)
        return pltpu.make_async_remote_copy(
            tr_ref.at[block], pt_ref.at[pl.ds(k * part, part)], pt_send, pt_recv,
            device_id=partner, device_id_type=MESH)

    for k in range(n_y):
        pt_copy(k).start()
    for k in range(n_y):
        block = pl.ds(pl.multiple_of((2 * lax.rem(y + k, n_y) + core) * part, 16), part)
        ot_ref[k * part:(k + 1) * part, :] = tr_ref[block, :]

    wait_bytes(vst_ref.at[pl.ds(0, n_t - 1)], vs_recv)
    verif_off = combine(vst_ref) - jnp.log(F32(0.8))
    for b in range(rows // LANES):
        at = slice(b * LANES, (b + 1) * LANES)
        b_ref[at, :] = to_columns(verif_off[b:b + 1]) - lw_ref[at, :]
    wait_bytes(dst_ref.at[pl.ds(0, n_t - 1)], ds_recv)
    draft_off = combine(dst_ref)
    for b in range(rows // LANES):
        at = slice(b * LANES, (b + 1) * LANES)
        a_ref[at, :] = to_columns(draft_off[b:b + 1]) - lw_ref[at, :]

    lane = lax.broadcasted_iota(jnp.int32, (64, LANES), 1)

    def grads(i):
        for b in range(rows // 64):
            at = slice(b * 64, (b + 1) * 64)
            for j in range(CHUNK // LANES):
                col = pl.ds(pl.multiple_of(i * CHUNK + j * LANES, LANES), LANES)
                draft = jnp.exp(g_ref[at, col].astype(F32) - a_ref[at, :])
                verif = jnp.exp(v_ref[at, col].astype(F32) - b_ref[at, :])
                hit = i_ref[at, :] - (i * CHUNK + j * LANES) == lane
                g_ref[at, col] = (draft - verif - jnp.where(hit, w_ref[at, :], 0.0)).astype(BF16)

    def g_copy(i):
        return pltpu.make_async_remote_copy(
            g_ref.at[:, columns(i)], gp_ref.at[:, columns(i)], g_send, g_recv.at[i],
            device_id=partner, device_id_type=MESH)

    def left(i):
        return pl.ds(pl.multiple_of(i * CHUNK, LANES), LANES)

    def right(i):
        return pl.ds(pl.multiple_of(i * CHUNK + LANES, LANES), LANES)

    def slab(k):
        return pl.ds(k * part, part)

    def y_copy(k, col, dst_ref, sem, to):
        return pltpu.make_async_remote_copy(
            p_ref.at[slab(k), col], dst_ref.at[:, col], y_send, sem, device_id=to, device_id_type=MESH)

    def product(i):
        p_ref[:, columns(i)] = (
            jnp.dot(ot_ref[...], g_ref[:, columns(i)], preferred_element_type=F32)
            + jnp.dot(pt_ref[...], gp_ref[:, columns(i)], preferred_element_type=F32)).astype(BF16)

    def far_sends(i):
        y_copy(2, left(i), f_ref, f_recv.at[i, 0], down).start()
        y_copy(2, right(i), f_ref, f_recv.at[i, 1], up).start()

    def near_sends(i):
        y_copy(1, left(i), o_ref, o_recv, up).start()
        y_copy(3, right(i), o_ref, o_recv, down).start()

    def product_of(k, i):
        rows_of = slice(k * part, (k + 1) * part)
        p_ref[rows_of, columns(i)] = (
            jnp.dot(ot_ref[rows_of, :], g_ref[:, columns(i)], preferred_element_type=F32)
            + jnp.dot(pt_ref[rows_of, :], gp_ref[:, columns(i)], preferred_element_type=F32)).astype(BF16)

    grads(0)
    g_copy(0).start()
    wait_bytes(pt_ref, pt_recv)
    grads(1)
    g_copy(1).start()
    g_copy(0).wait_recv()
    product_of(2, 0)
    far_sends(0)
    for k in (1, 3, 0):
        product_of(k, 0)
    near_sends(0)

    @pl.loop(2, chunks)
    def _(i):
        grads(i)
        g_copy(i).start()
        g_copy(i - 1).wait_recv()
        product(i - 1)
        far_sends(i - 1)
        near_sends(i - 1)

    g_copy(chunks - 1).wait_recv()
    product(chunks - 1)
    far_sends(chunks - 1)
    near_sends(chunks - 1)

    @pl.loop(0, depth // CHUNK)
    def _(n):
        block = pl.ds(pl.multiple_of(n * CHUNK, CHUNK), CHUNK)
        gn_ref[:, block] = lax.dot_general(
            g_ref[...], u_ref[block, :], (((1,), (1,)), ((), ())), preferred_element_type=F32).astype(BF16)

    @pl.loop(1, n_t)
    def _(k):
        peer = lax.rem(t + k, n_t)
        pltpu.make_async_remote_copy(
            gn_ref.at[pl.ds(pl.multiple_of(peer * owned, owned), owned)], gr_ref.at[k], n_send, n_recv,
            device_id=(dp, peer), device_id_type=MESH).start()

    def add_hop(i, side):
        k, col = (3, left(i)) if side == 0 else (1, right(i))
        p_ref[slab(k), col] = (p_ref[slab(k), col].astype(F32) + f_ref[:, col].astype(F32)).astype(BF16)
        y_copy(k, col, out_s, s_recv, down if side == 0 else up).start()

    @pl.loop(0, chunks)
    def _(i):
        y_copy(2, left(i), f_ref, f_recv.at[i, 0], down).wait_recv()
        add_hop(i, 0)
        y_copy(2, right(i), f_ref, f_recv.at[i, 1], up).wait_recv()
        add_hop(i, 1)

    wait_bytes(o_ref, o_recv)

    @pl.loop(0, chunks)
    def _(i):
        cols = columns(i)
        p_ref[slab(0), cols] = (p_ref[slab(0), cols].astype(F32) + o_ref[:, cols].astype(F32)).astype(BF16)

    a_copy = pltpu.make_async_copy(p_ref.at[slab(0)], out_a, a_sem)
    a_copy.start()

    wait_bytes(gr_ref.at[pl.ds(0, n_t - 1)], n_recv)
    own = pl.ds(pl.multiple_of(t * owned, owned), owned)
    grad = gn_ref[own, :].astype(F32)
    for k in range(1, n_t):
        grad += gr_ref[k].astype(F32)
    hidden = hid_ref[...].astype(F32)
    inverse = lax.rsqrt(jnp.mean(hidden * hidden, axis=-1, keepdims=True) + 1e-06)
    normed = hidden * inverse
    grad = grad * gain_ref[...][None, :]
    inner = jnp.mean(grad * normed, axis=-1, keepdims=True)
    out_h[...] = (inverse * (grad - normed * inner)).astype(BF16)

    a_copy.wait()
    wait_bytes(out_s, s_recv)
    for part_sent in (sc_ref.at[0], sc_ref.at[0], sc_ref.at[3], sc_ref.at[0, 0, pl.ds(0, 3)], sc_ref.at[0, 0, pl.ds(0, 3)]):
        wait_bytes(part_sent, ag_send)
    wait_bytes(vst_ref.at[pl.ds(0, n_t - 1)], vs_send)
    wait_bytes(dst_ref.at[pl.ds(0, n_t - 1)], ds_send)
    wait_bytes(pt_ref, pt_send)
    wait_bytes(g_ref, g_send)
    wait_bytes(p_ref.at[pl.ds(0, 3 * part)], y_send)
    wait_bytes(gr_ref.at[pl.ds(0, n_t - 1)], n_send)


def finish(own_ref, sent_ref, hid_ref, out_u, out_h):
    out_u[...] = (own_ref[...].astype(F32) + sent_ref[...].astype(F32)).astype(BF16)
    out_h[...] = hid_ref[...]


def body(n_dp, n_t, hidden, norm_gain, unembed, verifier_logits, served_ids, accepted):
    owned, depth = hidden.shape
    rows, width = verifier_logits.shape
    part = depth // n_dp
    chunks = width // CHUNK
    vmem = pl.BlockSpec(memory_space=pltpu.VMEM)
    hbm = pl.BlockSpec(memory_space=pl.ANY)
    dma = pltpu.SemaphoreType.DMA
    own, sent, grad_hidden = pl.pallas_call(
        functools.partial(kernel, n_dp, n_t),
        out_shape=(
            jax.ShapeDtypeStruct((part, width), BF16),
            jax.ShapeDtypeStruct((part, width), BF16),
            jax.ShapeDtypeStruct((owned, depth), BF16),
        ),
        in_specs=[vmem, vmem, hbm, hbm, vmem, vmem],
        out_specs=(hbm, hbm, vmem),
        scratch_shapes=[
            pltpu.VMEM((rows, CHUNK), F32),
            pltpu.VMEM((rows, CHUNK), F32),
            pltpu.VMEM((depth, width), BF16),
            pltpu.VMEM((rows, width), BF16),
            pltpu.VMEM((rows, width), BF16),
            pltpu.VMEM((rows, width), BF16),
            pltpu.VMEM((SIDE, 2, SIDE, owned // 2, depth), BF16),
            pltpu.VMEM((depth, rows), BF16),
            pltpu.VMEM((depth // 2, rows), BF16),
            pltpu.VMEM((depth // 2, rows), BF16),
            pltpu.VMEM((depth // 2, width), BF16),
            pltpu.VMEM((part, width), BF16),
            pltpu.VMEM((part, width), BF16),
            pltpu.VMEM((rows, depth), BF16),
            pltpu.VMEM((n_t, owned, depth), BF16),
            pltpu.VMEM((rows, LANES), F32),
            pltpu.VMEM((rows, LANES), F32),
            pltpu.VMEM((rows, LANES), F32),
            pltpu.VMEM((rows, LANES), jnp.int32),
            pltpu.VMEM((rows, LANES), F32),
            pltpu.VMEM((rows, LANES), F32),
            pltpu.VMEM((rows, LANES), F32),
            pltpu.VMEM((rows, LANES), F32),
            pltpu.VMEM((n_t, 8, LANES), F32),
            pltpu.VMEM((n_t, 8, LANES), F32),
            dma, dma((chunks,)), dma, dma((WAVES, 2, SIDE)), dma((WAVES, 2, SIDE, 2)), dma((WAVES,)), dma, dma, dma, dma, dma, dma,
            dma, dma((chunks,)), dma, dma((chunks, 2)), dma, dma, dma, dma, dma,
        ],
        compiler_params=pltpu.CompilerParams(
            collective_id=0, has_side_effects=True, vmem_limit_bytes=62 * 1024 * 1024),
        cost_estimate=pl.CostEstimate(
            flops=6 * rows * depth * width, bytes_accessed=2 * (depth + rows + part) * width,
            transcendentals=4 * rows * width),
    )(hidden, norm_gain, unembed, verifier_logits, served_ids.reshape(rows // LANES, LANES), accepted.reshape(1, rows // DRAFT))
    steps = 3
    block = pl.BlockSpec((part // steps, width), lambda i: (i, 0))
    small = pl.BlockSpec((owned, depth), lambda i: (0, 0))
    return pl.pallas_call(
        finish,
        grid=(steps,),
        out_shape=(
            jax.ShapeDtypeStruct((part, width), BF16),
            jax.ShapeDtypeStruct((owned, depth), BF16),
        ),
        in_specs=[block, block, small],
        out_specs=(block, small),
        compiler_params=pltpu.CompilerParams(vmem_limit_bytes=62 * 1024 * 1024),
    )(own, sent, grad_hidden)


def solution(mesh):
    n_dp, n_t = mesh.shape["dp"], mesh.shape["tensor"]

    def run(*args):
        return body(n_dp, n_t, *args)

    return jax.shard_map(
        run,
        mesh=mesh,
        in_specs=(
            P(("dp", "tensor"), None),
            P(),
            P(None, "tensor"),
            P("dp", "tensor"),
            P("dp"),
            P("dp"),
        ),
        out_specs=(P("dp", "tensor"), P(("dp", "tensor"), None)),
        check_vma=False,
    )
```
